32 devices in a mesh: narrow: 4 (over y, x), wide: 8 (over z, core).
Axes of the slice: x: 2, y: 2, z: 4, core: 2. Of those that a mesh axis runs over, the one named last changes fastest.
Arguments:
- lengths: int32 [32], P(('narrow', 'wide')), may hold values from 40 to 512, as said below
- char_ids: int32 [32, 512, 50], P(('narrow', 'wide')), may hold values from 0 to 261
- char_counts: int32 [32, 512], P(('narrow', 'wide')), may hold values from 1 to 50
- token_types: int32 [32, 512], P(('narrow', 'wide')), may hold values from 0 to 1
- out_grad: bfloat16 [32, 512, 768], P(('narrow', 'wide')), may hold values from -6 to 6
- char_table: bfloat16 [4192], P('wide'), may hold values from -6 to 6
- conv_1: bfloat16 [16, 32], P(None, 'wide'), may hold values from -1.5 to 1.5
- conv_2: bfloat16 [32, 32], P(None, 'wide'), may hold values from -1 to 1
- conv_3: bfloat16 [48, 64], P(None, 'wide'), may hold values from -0.875 to 0.875
- conv_4: bfloat16 [64, 128], P(None, 'wide'), may hold values from -0.75 to 0.75
- conv_5: bfloat16 [80, 256], P(None, 'wide'), may hold values from -0.625 to 0.625
- conv_6: bfloat16 [96, 512], P(None, 'wide'), may hold values from -0.625 to 0.625
- conv_7: bfloat16 [112, 1024], P(None, 'wide'), may hold values from -0.5 to 0.5
- conv_bias: bfloat16 [2048], P('wide'), may hold values from -2 to 2
- highway_weight: bfloat16 [2, 2048, 4096], P(None, 'wide'), may hold values from -0.125 to 0.125
- highway_bias: bfloat16 [2, 4096], P(None, 'wide'), may hold values from -2 to 2
- projection: bfloat16 [2048, 768], P('wide'), may hold values from -0.125 to 0.125
- position_table: bfloat16 [512, 768], P('wide'), may hold values from -3 to 3
- type_table: bfloat16 [2, 768], P(None, 'wide'), may hold values from -3 to 3
- embed_gain: bfloat16 [768], P('wide'), may hold values from 0.5 to 1.5
- embed_biases: bfloat16 [2, 768], P(None, 'wide'), may hold values from -2 to 2
- qkv_weight: bfloat16 [768, 2304], P('wide'), may hold values from -0.21875 to 0.21875
- out_weight: bfloat16 [768, 768], P('wide'), may hold values from -0.875 to 0.875
- ff_in: bfloat16 [768, 3072], P('wide'), may hold values from -0.21875 to 0.21875
- ff_in_bias: bfloat16 [3072], P('wide'), may hold values from -2 to 2
- ff_out: bfloat16 [3072, 768], P('wide'), may hold values from -0.109375 to 0.109375
- layer_gains: bfloat16 [2, 768], P(None, 'wide'), may hold values from 0.5 to 1.5
- layer_biases: bfloat16 [6, 768], P(None, 'wide'), may hold values from -2 to 2
Outputs:
- hidden_out: float32 [32, 512, 768], P(('narrow', 'wide'))
- grad_char_table: float32 [4192], P('wide')
- grad_conv_1: float32 [16, 32], P(None, 'wide')
- grad_conv_2: float32 [32, 32], P(None, 'wide')
- grad_conv_3: float32 [48, 64], P(None, 'wide')
- grad_conv_4: float32 [64, 128], P(None, 'wide')
- grad_conv_5: float32 [80, 256], P(None, 'wide')
- grad_conv_6: float32 [96, 512], P(None, 'wide')
- grad_conv_7: float32 [112, 1024], P(None, 'wide')
- grad_conv_bias: float32 [2048], P('wide')
- grad_highway_weight: float32 [2, 2048, 4096], P(None, 'wide')
- grad_highway_bias: float32 [2, 4096], P(None, 'wide')
- grad_projection: float32 [2048, 768], P('wide')
- grad_position_table: float32 [512, 768], P('wide')
- grad_type_table: float32 [2, 768], P(None, 'wide')
- grad_embed_gain: float32 [768], P('wide')
- grad_embed_biases: float32 [2, 768], P(None, 'wide')
- grad_qkv_weight: float32 [768, 2304], P('wide')
- grad_out_weight: float32 [768, 768], P('wide')
- grad_ff_in: float32 [768, 3072], P('wide')
- grad_ff_in_bias: float32 [3072], P('wide')
- grad_ff_out: float32 [3072, 768], P('wide')
- grad_layer_gains: float32 [2, 768], P(None, 'wide')
- grad_layer_biases: float32 [6, 768], P(None, 'wide')
The draws below stay inside these ranges and needn't reach their ends.
Inputs may be any that keep to these rules, and one draw needn't show every extreme that they name: `lengths`: words of each sequence; at least one sequence has 512 words and one has 40.
All inputs are finite; a program needn't handle non-finite values.
Results may differ from the reference program's by a relative error of at most 0.024.
Values may be sent and summed in bfloat16 or wider, within the bound.
No kernel may reach another device: no remote copies, remote signals or barrier semaphores. Data moves between devices by JAX's collectives and lax.ppermute only.
A program may use at most 384 MiB of HBM per device.

```python
import math
import jax
import jax.numpy as jnp
from jax import lax

D = 768
HEADS = 12
HDIM = 64
FF = 3072
CHARS = 262
CDIM = 16
WCHARS = 50
CH1 = 32
CH2 = 32
CH3 = 64
CH4 = 128
CH5 = 256
CH6 = 512
CH7 = 1024
LEN = 512
MINLEN = 40
FILT = 2048
SEQS = 32


def draw_lengths(key, part):
    key = jax.random.fold_in(key, 11)
    pick_key, other_key, base_key = jax.random.split(key, 3)
    values_drawn = jax.random.randint(base_key, (SEQS,), MINLEN, LEN + 1)
    longest = jax.random.randint(pick_key, (), 0, SEQS)
    shortest = (longest + 1 + jax.random.randint(other_key, (), 0, SEQS - 1)) % SEQS
    values_drawn = values_drawn.at[longest].set(LEN)
    values_drawn = values_drawn.at[shortest].set(MINLEN)
    return values_drawn.astype(jnp.int32)


def touch_ends(array, key, least, largest):
    place = [jax.random.randint(jax.random.fold_in(key, axis), (), 0, length) for axis, length in enumerate(array.shape)]
    widest = array.shape.index(max(array.shape))
    neighbour = place[:widest] + [(place[widest] + 1) % array.shape[widest]] + place[widest + 1:]
    return array.at[tuple(place)].set(least).at[tuple(neighbour)].set(largest)


def block_levels(rng, shape, cuts, least, top_value):
    loudness, own = 1.0, jax.random.fold_in(rng, 6)
    for position, shards_of in cuts:
        draws = jnp.exp(jax.random.uniform(jax.random.fold_in(own, position), (shards_of,), jnp.float32, least / len(cuts), top_value / len(cuts)))
        loudness = loudness * jnp.repeat(draws, shape[position] // shards_of).reshape([-1 if axis == position else 1 for axis in range(len(shape))])
    return loudness


def normal_values(rng, shape, scale, most, cuts=(), kind=jnp.bfloat16):
    result = scale * jax.random.normal(rng, shape, jnp.float32)
    if cuts:
        result = result * block_levels(rng, shape, cuts, -0.22, 0.18)
    return jnp.clip(result, -most, most).astype(kind)


def setup_inputs(seed: int = 0) -> dict:
    streams_of = jax.random.split(jax.random.key(seed), 29)
    lengths = draw_lengths(jax.random.fold_in(streams_of[28], 71), 0)
    char_ids = touch_ends(jax.random.randint(streams_of[1], (SEQS, LEN, WCHARS), 0, CHARS), jax.random.fold_in(streams_of[1], 1), 0, CHARS - 1).astype(jnp.int32)
    char_counts = touch_ends(jax.random.randint(streams_of[2], (SEQS, LEN), 1, WCHARS + 1), jax.random.fold_in(streams_of[2], 1), 1, WCHARS).astype(jnp.int32)
    token_types = touch_ends(jax.random.randint(streams_of[3], (SEQS, LEN), 0, 2), jax.random.fold_in(streams_of[3], 1), 0, 1).astype(jnp.int32)
    out_grad = normal_values(streams_of[4], (SEQS, LEN, D), 1.0, 6.0, ((0, 32),))
    char_table = normal_values(streams_of[5], (CHARS * CDIM,), 1.0, 6.0, ((0, 8),))
    conv_1 = normal_values(streams_of[6], (CDIM, CH1), CDIM ** -0.5, 1.5, ((1, 8),))
    conv_2 = normal_values(streams_of[7], (2 * CDIM, CH2), (2 * CDIM) ** -0.5, 1.0, ((1, 8),))
    conv_3 = normal_values(streams_of[8], (3 * CDIM, CH3), (3 * CDIM) ** -0.5, 0.875, ((1, 8),))
    conv_4 = normal_values(streams_of[9], (4 * CDIM, CH4), (4 * CDIM) ** -0.5, 0.75, ((1, 8),))
    conv_5 = normal_values(streams_of[10], (5 * CDIM, CH5), (5 * CDIM) ** -0.5, 0.625, ((1, 8),))
    conv_6 = normal_values(streams_of[11], (6 * CDIM, CH6), (6 * CDIM) ** -0.5, 0.625, ((1, 8),))
    conv_7 = normal_values(streams_of[12], (7 * CDIM, CH7), (7 * CDIM) ** -0.5, 0.5, ((1, 8),))
    conv_bias = normal_values(streams_of[13], (FILT,), 0.3, 2.0, ((0, 8),))
    highway_weight = normal_values(streams_of[14], (2, FILT, 2 * FILT), FILT ** -0.5, 0.125, ((1, 8),))
    highway_bias = normal_values(streams_of[15], (2, 2 * FILT), 0.3, 2.0, ((1, 8),))
    projection = normal_values(streams_of[16], (FILT, D), FILT ** -0.5, 0.125, ((0, 8),))
    position_table = normal_values(streams_of[17], (LEN, D), 0.5, 3.0, ((0, 8),))
    type_table = normal_values(streams_of[18], (2, D), 0.5, 3.0, ((1, 8),))
    embed_gain = jnp.clip(1.0 + 0.1 * jax.random.normal(streams_of[19], (D,), jnp.float32), 0.5, 1.5).astype(jnp.bfloat16)
    embed_biases = normal_values(streams_of[20], (2, D), 0.3, 2.0, ((1, 8),))
    qkv_weight = normal_values(streams_of[21], (D, 3 * D), D ** -0.5, 0.21875, ((0, 8),))
    out_weight = normal_values(streams_of[22], (D, D), (D // 16) ** -0.5, 0.875, ((0, 8),))
    ff_in = normal_values(streams_of[23], (D, FF), D ** -0.5, 0.21875, ((0, 8),))
    ff_in_bias = normal_values(streams_of[24], (FF,), 0.3, 2.0, ((0, 8),))
    ff_out = normal_values(streams_of[25], (FF, D), FF ** -0.5, 0.109375, ((0, 8),))
    layer_gains = jnp.clip(1.0 + 0.1 * jax.random.normal(streams_of[26], (2, D), jnp.float32), 0.5, 1.5).astype(jnp.bfloat16)
    layer_biases = normal_values(streams_of[27], (6, D), 0.3, 2.0, ((1, 8),))
    return dict(lengths=lengths, char_ids=char_ids, char_counts=char_counts, token_types=token_types, out_grad=out_grad, char_table=char_table, conv_1=conv_1, conv_2=conv_2, conv_3=conv_3, conv_4=conv_4, conv_5=conv_5, conv_6=conv_6, conv_7=conv_7, conv_bias=conv_bias, highway_weight=highway_weight, highway_bias=highway_bias, projection=projection, position_table=position_table, type_table=type_table, embed_gain=embed_gain, embed_biases=embed_biases, qkv_weight=qkv_weight, out_weight=out_weight, ff_in=ff_in, ff_in_bias=ff_in_bias, ff_out=ff_out, layer_gains=layer_gains, layer_biases=layer_biases)


@jax.custom_vjp
def low(v):
    return lax.optimization_barrier(v.astype(jnp.bfloat16)).astype(jnp.float32)

@jax.custom_vjp
def low_back(v):
    return v

def low_keep(v):
    return (low(v), None)

def low_pass(kept, grad):
    return (grad,)

def back_keep(v):
    return (v, None)

def back_low(kept, grad):
    return (low(grad),)
low.defvjp(low_keep, low_pass)
low_back.defvjp(back_keep, back_low)
EPSILON = 1e-06
MASKED_SCORE = -1e+30
ROOT_HALF = 0.7071067811865476

def gelu_curve(value):
    return 0.5 * value * (1.0 + lax.erf(value * ROOT_HALF))

def normalize(value, gain, shift):
    average = lax.optimization_barrier(jnp.mean(value, axis=-1, keepdims=True))
    centred = value - average
    spread = lax.optimization_barrier(jnp.mean(centred * centred, axis=-1, keepdims=True))
    return centred * lax.rsqrt(spread + EPSILON) * gain + shift

def seq_forward(weights, seq_chars, seq_counts, seq_types, seq_length):
    table_rows = weights[0].reshape(CHARS, CDIM)
    present = (jnp.arange(WCHARS, dtype=jnp.int32)[None, :] < seq_counts[:, None]).astype(jnp.float32)
    char_vecs = low_back(table_rows[seq_chars] * present[:, :, None])
    pieces = []
    channel_start = 0
    for kernel in weights[1:8]:
        window = kernel.shape[0] // CDIM
        channels = kernel.shape[1]
        extent = WCHARS - window + 1
        kernel_taps = kernel.reshape(window, CDIM, channels)
        summed = jnp.zeros((LEN, extent, channels), jnp.float32) + weights[8][channel_start:channel_start + channels]
        for offset in range(window):
            summed = summed + jnp.einsum('tpd,dh->tph', char_vecs[:, offset:offset + extent], kernel_taps[offset], precision=lax.Precision.HIGHEST)
        summed = low_back(summed)
        limit = jnp.maximum(seq_counts - window, 0)
        valid = (jnp.arange(extent, dtype=jnp.int32)[None, :] <= limit[:, None]).astype(jnp.float32)
        denominator = lax.optimization_barrier(jnp.sum(jnp.exp(summed) * valid[:, :, None], axis=1))
        pieces.append(jnp.log(denominator / (limit + 1).astype(jnp.float32)[:, None]))
        channel_start += channels
    carried = gelu_curve(jnp.concatenate(pieces, axis=1))
    for number in range(2):
        mixing = low_back(jnp.dot(low(carried), weights[9][number], precision=lax.Precision.HIGHEST) + weights[10][number])
        gate_part = jax.nn.sigmoid(mixing[:, FILT:])
        carried = gate_part * carried + (1.0 - gate_part) * gelu_curve(mixing[:, :FILT])
    embed_sum = low_back(jnp.dot(low(carried), weights[11], precision=lax.Precision.HIGHEST) + weights[15][0] + weights[12] + weights[13][seq_types])
    embedded = normalize(embed_sum, weights[14], weights[15][1])
    shift_rows = weights[22]
    gain_rows = weights[21]
    bias_full = jnp.concatenate([shift_rows[0], jnp.zeros_like(shift_rows[0]), shift_rows[1]])
    projected = low_back(low(jnp.dot(low(embedded), weights[16], precision=lax.Precision.HIGHEST) + bias_full))
    heads_all = projected.reshape(LEN, 3, HEADS, HDIM)
    scale_factor = 1.0 / math.sqrt(HDIM)
    scores = low_back(jnp.einsum('qhe,khe->hqk', heads_all[:, 0], heads_all[:, 1], precision=lax.Precision.HIGHEST) * scale_factor)
    keep_keys = jnp.arange(LEN, dtype=jnp.int32) < seq_length
    scores = jnp.where(keep_keys[None, None, :], scores, MASKED_SCORE)
    highest = lax.optimization_barrier(jnp.max(scores, axis=-1, keepdims=True))
    exponent = jnp.exp(scores - highest)
    attention = exponent / lax.optimization_barrier(jnp.sum(exponent, axis=-1, keepdims=True))
    context = low_back(low(jnp.einsum('hqk,khe->qhe', low(attention), heads_all[:, 2], precision=lax.Precision.HIGHEST).reshape(LEN, D)))
    attn_out = low_back(jnp.dot(context, weights[17], precision=lax.Precision.HIGHEST) + shift_rows[2])
    first_out = normalize(embedded + attn_out, gain_rows[0], shift_rows[3])
    inner_pre = low_back(jnp.dot(low(first_out), weights[18], precision=lax.Precision.HIGHEST) + weights[19])
    ffn_out = low_back(jnp.dot(low(gelu_curve(inner_pre)), weights[20], precision=lax.Precision.HIGHEST) + shift_rows[4])
    final_out = normalize(first_out + ffn_out, gain_rows[1], shift_rows[5])
    row_keep = (jnp.arange(LEN, dtype=jnp.int32) < seq_length).astype(jnp.float32)
    return final_out * row_keep[:, None]

def reference(lengths, char_ids, char_counts, token_types, out_grad, char_table, conv_1, conv_2, conv_3, conv_4, conv_5, conv_6, conv_7, conv_bias, highway_weight, highway_bias, projection, position_table, type_table, embed_gain, embed_biases, qkv_weight, out_weight, ff_in, ff_in_bias, ff_out, layer_gains, layer_biases):
    weights = tuple((argument.astype(jnp.float32) for argument in (char_table, conv_1, conv_2, conv_3, conv_4, conv_5, conv_6, conv_7, conv_bias, highway_weight, highway_bias, projection, position_table, type_table, embed_gain, embed_biases, qkv_weight, out_weight, ff_in, ff_in_bias, ff_out, layer_gains, layer_biases)))

    def whole_batch(params):

        def single(inputs):
            return jax.checkpoint(seq_forward)(params, inputs[0], inputs[1], inputs[2], inputs[3])
        return lax.map(single, (char_ids, char_counts, token_types, lengths))
    hidden_out, pullback = jax.vjp(whole_batch, weights)
    gradients = pullback(out_grad.astype(jnp.float32))[0]
    return (hidden_out, gradients[0], gradients[1], gradients[2], gradients[3], gradients[4], gradients[5], gradients[6], gradients[7], gradients[8], gradients[9], gradients[10], gradients[11], gradients[12], gradients[13], gradients[14], gradients[15], gradients[16], gradients[17], gradients[18], gradients[19], gradients[20], gradients[21], gradients[22])
```

```python
import functools
import math

import jax
import jax.numpy as jnp
from jax import lax
from jax.experimental import pallas as pl
from jax.experimental.pallas import tpu as pltpu
from jax.sharding import PartitionSpec as P

HEADS = 12
HDIM = 64
CDIM = 16
WCH = 50
TAP = 112
KROWS = 128
MASK_LOW = -1e30
VPAD = 384
VROWS = 272
FLAT = 896
CONV_BLOCK = 128

EPSILON = 1e-06
MASKED_SCORE = -1e30
ROOT_HALF = 0.7071067811865476
NORMAL_PEAK = 0.3989422804014327
CONTRACT_ROWS = (((0,), (0,)), ((), ()))
CONTRACT_COLS = (((1,), (1,)), ((), ()))
INNER_FIRST = (((1,), (0,)), ((), ()))


def gelu_curve(value):
    return 0.5 * value * (1.0 + lax.erf(value * ROOT_HALF))


def gelu_slope(value):
    return 0.5 * (1.0 + lax.erf(value * ROOT_HALF)) + value * NORMAL_PEAK * jnp.exp(
        -0.5 * value * value
    )


def normalize(value, gain, shift):
    average = jnp.mean(value, axis=-1, keepdims=True)
    centred = value - average
    spread = jnp.mean(centred * centred, axis=-1, keepdims=True)
    return centred * lax.rsqrt(spread + EPSILON) * gain + shift


def matmul(left, right, dims=INNER_FIRST):
    return lax.dot_general(left, right, dims, preferred_element_type=jnp.float32)


def conv_fwd_body(block, filters, held, ids_ref, cnt_ref, table_ref, kern_ref, *rest):
    x_ref, den_ref, flat, hot = rest[held:]
    lane = lax.broadcasted_iota(jnp.int32, (block, VPAD), 1)
    groups = FLAT // 128
    for turn in range(8):
        for g in range(groups):
            slot = 8 * g + turn
            if slot < WCH:
                col = ids_ref[:, slot:slot + 1]
                hot[g * block:(g + 1) * block, :] = (col == lane).astype(jnp.float32).astype(jnp.bfloat16)
            else:
                hot[g * block:(g + 1) * block, :] = jnp.zeros((block, VPAD), jnp.bfloat16)
        found = matmul(hot[...], table_ref[turn])
        for g in range(groups):
            part = found[g * block:(g + 1) * block, :]
            if turn == 0:
                flat[:, g * 128:(g + 1) * 128] = part
            else:
                flat[:, g * 128:(g + 1) * 128] += part
    flat[:, FLAT:] = jnp.zeros((block, 128), jnp.float32)
    lane_x = lax.broadcasted_iota(jnp.int32, (block, KROWS), 1)
    width = lane_x - TAP
    count = jnp.broadcast_to(cnt_ref[...], (block, KROWS))
    reach = jnp.maximum(count, width)
    for place in range(WCH):
        a, r = divmod(place, 8)
        first = flat[:, a * 128:(a + 1) * 128]
        if r:
            second = flat[:, (a + 1) * 128:(a + 2) * 128]
            first = pltpu.roll(first, 128 - 16 * r, 1)
            second = pltpu.roll(second, 128 - 16 * r, 1)
            first = jnp.where(lane_x < 128 - 16 * r, first, second)
        extra = jnp.where(width == 0, 1.0, jnp.where((width <= 7) & (place + width > reach), MASK_LOW, 0.0))
        x_ref[place * block:(place + 1) * block, :] = jnp.where(width < 0, first, extra).astype(jnp.bfloat16)

    step = 4
    den_ref[...] = jnp.zeros_like(den_ref)
    tile = 512

    def piece(start, count_p, lo, hi):
        rows = x_ref[pl.ds(start, count_p * block), :]
        summed = matmul(rows, kern_ref[:, lo:hi])
        e = jnp.exp(summed)
        total = e[:block]
        for i in range(1, count_p):
            total = total + e[i * block:(i + 1) * block]
        den_ref[:, lo:hi] += total

    def chunk(i, carry):
        start = pl.multiple_of(i * step * block, step * block)
        for lo in range(0, filters, tile):
            piece(start, step, lo, lo + tile)
        return carry

    lax.fori_loop(0, 11, chunk, 0)
    for lo in range(0, 1024, tile):
        piece(44 * block, 4, lo, lo + tile)
    piece(48 * block, 2, 0, 256)


def conv_forward(call, ids, counts, tables, kern, state):
    block = CONV_BLOCK
    words, filters = ids.shape[0], kern.shape[1]
    return pl.pallas_call(
        functools.partial(conv_fwd_body, block, filters, len(state)),
        grid=(1,),
        in_specs=[
            pl.BlockSpec((block, ids.shape[1]), lambda i: (call, 0)),
            pl.BlockSpec((block, 1), lambda i: (call, 0)),
            pl.BlockSpec(tables.shape, lambda i: (0, 0, 0)),
            pl.BlockSpec(kern.shape, lambda i: (0, 0)),
        ]
        + [pl.BlockSpec(memory_space=pl.ANY)] * len(state),
        out_specs=[
            pl.BlockSpec((WCH * block, KROWS), lambda i: (call, 0)),
            pl.BlockSpec((block, filters), lambda i: (call, 0)),
        ],
        out_shape=[
            jax.ShapeDtypeStruct((words * WCH, KROWS), jnp.bfloat16),
            jax.ShapeDtypeStruct((words, filters), jnp.float32),
        ],
        input_output_aliases={4: 0, 5: 1} if state else {},
        scratch_shapes=[
            pltpu.VMEM((block, FLAT + 128), jnp.float32),
            pltpu.VMEM((FLAT // 128 * block, VPAD), jnp.bfloat16),
        ],
        compiler_params=pltpu.CompilerParams(vmem_limit_bytes=40 << 20),
        cost_estimate=pl.CostEstimate(
            flops=block * WCH * 32 * filters,
            bytes_accessed=block * filters,
            transcendentals=0,
        ),
        name="conv_forward",
    )(ids, counts, tables, kern, *state)


def conv_bwd_body(block, filters, idst_ref, x_ref, ginv_ref, kern_ref, kern_in_ref, table_in_ref, kern_grad_ref, table_grad_ref, gx, flat, hot, part):
    kern_grad_ref[...] = kern_in_ref[...]
    table_grad_ref[...] = table_in_ref[...]

    tile = 512
    step = 4

    def piece(start, count_p, lo, hi):
        rows = x_ref[pl.ds(start, count_p * block), :]
        k = kern_ref[:, lo:hi]
        e = jnp.exp(matmul(rows, k))
        scale = ginv_ref[:, lo:hi]
        g = jnp.concatenate([e[i * block:(i + 1) * block] * scale for i in range(count_p)], axis=0).astype(jnp.bfloat16)
        kern_grad_ref[:, lo:hi] += matmul(rows, g, CONTRACT_ROWS)
        return matmul(g, k, CONTRACT_COLS)

    def chunk(i, carry):
        start = pl.multiple_of(i * step * block, step * block)
        total = piece(start, step, 0, tile)
        for lo in range(tile, filters, tile):
            total = total + piece(start, step, lo, lo + tile)
        gx[pl.ds(start, step * block), :] = total
        return carry

    lax.fori_loop(0, 11, chunk, 0)
    gx[44 * block:48 * block, :] = piece(44 * block, 4, 0, 512) + piece(44 * block, 4, 512, 1024)
    gx[48 * block:50 * block, :] = piece(48 * block, 2, 0, 256)

    flat[...] = jnp.zeros_like(flat)
    lane_x = lax.broadcasted_iota(jnp.int32, (block, 128), 1)
    for place in range(WCH):
        a, r = divmod(place, 8)
        value = jnp.where(lane_x < TAP, gx[place * block:(place + 1) * block, :], 0.0)
        if r:
            value = pltpu.roll(value, 16 * r, 1)
            flat[:, a * 128:(a + 1) * 128] += jnp.where(lane_x >= 16 * r, value, 0.0)
            flat[:, (a + 1) * 128:(a + 2) * 128] += jnp.where(lane_x < 16 * r, value, 0.0)
        else:
            flat[:, a * 128:(a + 1) * 128] += value
    groups = FLAT // 128
    for g in range(groups):
        part[g * block:(g + 1) * block, :] = flat[:, g * 128:(g + 1) * 128].astype(jnp.bfloat16)
    sub = lax.broadcasted_iota(jnp.int32, (VROWS, block), 0)
    lane_t = lax.broadcasted_iota(jnp.int32, (VROWS, 128), 1)
    for turn in range(8):
        for g in range(groups):
            slot = 8 * g + turn
            if slot < WCH:
                row = idst_ref[slot:slot + 1, :]
                hot[:, g * block:(g + 1) * block] = (row == sub).astype(jnp.float32).astype(jnp.bfloat16)
            else:
                hot[:, g * block:(g + 1) * block] = jnp.zeros((VROWS, block), jnp.bfloat16)
        found = matmul(hot[...], part[...])
        table_grad_ref[...] += jnp.where((lane_t >= 16 * turn) & (lane_t < 16 * turn + 16), found, 0.0)


def conv_backward(call, ids_t, x, ginv, kern, state):
    block = CONV_BLOCK
    filters = ginv.shape[1]
    whole = [pl.BlockSpec(kern.shape, lambda i: (0, 0)), pl.BlockSpec((VROWS, 128), lambda i: (0, 0))]
    return pl.pallas_call(
        functools.partial(conv_bwd_body, block, filters),
        grid=(1,),
        in_specs=[
            pl.BlockSpec((ids_t.shape[0], block), lambda i: (0, call)),
            pl.BlockSpec((WCH * block, KROWS), lambda i: (call, 0)),
            pl.BlockSpec((block, filters), lambda i: (call, 0)),
            pl.BlockSpec(kern.shape, lambda i: (0, 0)),
        ]
        + whole,
        out_specs=whole,
        out_shape=[
            jax.ShapeDtypeStruct(kern.shape, jnp.float32),
            jax.ShapeDtypeStruct((VROWS, 128), jnp.float32),
        ],
        input_output_aliases={4: 0, 5: 1},
        scratch_shapes=[
            pltpu.VMEM((WCH * block, 128), jnp.float32),
            pltpu.VMEM((block, FLAT + 128), jnp.float32),
            pltpu.VMEM((VROWS, FLAT // 128 * block), jnp.bfloat16),
            pltpu.VMEM((FLAT // 128 * block, 128), jnp.bfloat16),
        ],
        compiler_params=pltpu.CompilerParams(vmem_limit_bytes=40 << 20),
        cost_estimate=pl.CostEstimate(
            flops=block * WCH * 64 * filters,
            bytes_accessed=block * filters,
            transcendentals=0,
        ),
        name="conv_backward",
    )(ids_t, x, ginv, kern, *state)


def table_turns(table):
    padded = jnp.pad(table, ((0, VPAD - table.shape[0]), (0, 0)))
    return jnp.stack([jnp.pad(padded, ((0, 0), (16 * r, 112 - 16 * r))) for r in range(8)])


def score_block(heads_all, length):
    seq_len = heads_all.shape[0]
    scale_factor = 1.0 / math.sqrt(HDIM)
    scores = (
        jnp.einsum(
            "qhe,khe->hqk", heads_all[:, 0], heads_all[:, 1], preferred_element_type=jnp.float32
        )
        * scale_factor
    )
    keep_keys = lax.broadcasted_iota(jnp.int32, (1, 1, seq_len), 2) < length
    return jnp.where(keep_keys, scores, MASKED_SCORE)


def attend(proj_seq, length):
    seq_len = proj_seq.shape[0]
    heads_all = proj_seq.reshape(seq_len, 3, HEADS, HDIM)
    scores = score_block(heads_all, length)
    highest = jnp.max(scores, axis=2, keepdims=True)
    exponent = jnp.exp(scores - highest)
    denominator = jnp.sum(exponent, axis=2, keepdims=True)
    attention = (exponent / denominator).astype(jnp.bfloat16)
    context = jnp.einsum(
        "hqk,khe->qhe", attention, heads_all[:, 2], preferred_element_type=jnp.float32
    )
    return (context.reshape(seq_len, -1).astype(jnp.bfloat16), highest + jnp.log(denominator))


def attend_back(proj_seq, log_total, grad_context, length):
    seq_len = proj_seq.shape[0]
    scale_factor = 1.0 / math.sqrt(HDIM)
    heads_all = proj_seq.reshape(seq_len, 3, HEADS, HDIM)
    grad_heads = grad_context.reshape(seq_len, HEADS, HDIM)
    attention = jnp.exp(score_block(heads_all, length) - log_total)
    grad_attention = jnp.einsum(
        "qhe,khe->hqk", grad_heads, heads_all[:, 2], preferred_element_type=jnp.float32
    )
    grad_values = jnp.einsum(
        "hqk,qhe->khe",
        attention.astype(jnp.bfloat16),
        grad_heads,
        preferred_element_type=jnp.float32,
    )
    row_dot = jnp.sum(attention * grad_attention, axis=2, keepdims=True)
    grad_scores = (attention * (grad_attention - row_dot)).astype(jnp.bfloat16)
    grad_queries = (
        jnp.einsum("hqk,khe->qhe", grad_scores, heads_all[:, 1], preferred_element_type=jnp.float32)
        * scale_factor
    )
    grad_keys = (
        jnp.einsum("hqk,qhe->khe", grad_scores, heads_all[:, 0], preferred_element_type=jnp.float32)
        * scale_factor
    )
    return (
        jnp.stack([grad_queries, grad_keys, grad_values], axis=1)
        .reshape(seq_len, -1)
        .astype(jnp.bfloat16)
    )


def core_swap(value, wide):
    return lax.ppermute(value, "wide", [(i, i ^ 1) for i in range(wide)])


def chip_shift(value, wide, step):
    return lax.ppermute(value, "wide", [(i, (i + 2 * step) % wide) for i in range(wide)])


def hop(value, narrow, bit):
    return lax.ppermute(value, "narrow", [(i, i ^ bit) for i in range(narrow)])


def low_bit(mask):
    return mask & -mask


def high_bit(mask):
    return 1 << (mask.bit_length() - 1)


def masks_of(narrow, level):
    return [mask for mask in range(narrow) if bin(mask).count("1") == level]


def levels_of(narrow):
    return range(1, narrow.bit_length())


def spread_level(known, narrow, level):
    for mask in masks_of(narrow, level):
        if level == 1:
            known[mask] = hop(known[0], narrow, mask)
        else:
            high, low = high_bit(mask), low_bit(mask)
            known[mask] = (hop(known[mask ^ high][0], narrow, high), hop(known[mask ^ low][1], narrow, low))


def add_low(left, right):
    return (left.astype(jnp.float32) + right.astype(jnp.float32)).astype(jnp.bfloat16)


def bits_of(narrow, half):
    bits = [1 << i for i in range(narrow.bit_length() - 1)]
    return bits if half else bits[::-1]


def sides(half, count):
    if half:
        return slice(1, count, 2), slice(0, count, 2)
    return slice(count // 2, count), slice(0, count // 2)


def collect_round(terms, narrow, turn):
    following = []
    for half, (parts, arrived) in enumerate(terms):
        leaving, staying = sides(half, parts.shape[0])
        sent = hop(add_low(parts[leaving], arrived[leaving]), narrow, bits_of(narrow, half)[turn])
        following.append((add_low(parts[staying], arrived[staying]), sent))
    return following


def tie(*groups):
    return lax.optimization_barrier(groups)


def own_columns(shard, place, narrow):
    rows, columns = shard.shape
    part = columns // 2 // narrow
    return jnp.stack(
        [lax.dynamic_slice(shard, (0, half * (columns // 2) + place * part), (rows, part)) for half in range(2)]
    )


def chip_groups(wide):
    return [[2 * chip + core for chip in range(wide // 2)] for core in range(2)]


def gather_chips(own, wide):
    return lax.all_gather(own, "wide", axis=0, tiled=False, axis_index_groups=chip_groups(wide))


def other_chips(value, chip):
    chips = value.shape[0]
    pieces = [
        lax.dynamic_index_in_dim(value, lax.rem(chip + chips - step, chips), 0, keepdims=False) for step in range(1, chips)
    ]
    return jnp.concatenate(pieces, axis=1)


def swap_known(known, narrow, wide):
    return core_swap(jnp.stack([jnp.stack(known[m]) if m & (m - 1) else known[m] for m in range(narrow)]), wide)


def weight_copies(narrow, layer, where_ref, mask, shard_ref, twin_ref, mine, other, slot_ref, sems):
    rows = shard_ref.shape[1]
    part = slot_ref.shape[2]
    filters = part * narrow
    chips = slot_ref.shape[1] // (2 * rows)
    copies = []
    for half in range(2):
        column = pl.multiple_of(half * filters + (where_ref[0] ^ mask) * part, part)
        for side, (near, far) in enumerate(((shard_ref, mine), (twin_ref, other))):
            for step in range(chips):
                src = near.at[layer, :, pl.ds(column, part)]
                if step:
                    src = far(mask, half).at[(step - 1) * rows : step * rows, :]
                copies.append((src, slot_ref.at[half, pl.ds(block_start(where_ref, side, step, chips, rows), rows), :]))
    return [pltpu.make_async_copy(src, dst, sems.at[i]) for i, (src, dst) in enumerate(copies)]


def block_start(where_ref, side, step, chips, rows):
    block = lax.rem(where_ref[1] + (chips - step), chips) * 2 + (where_ref[2] ^ side)
    return pl.multiple_of(block * rows, rows)


def weights_of_step(narrow, layer, where_ref, shard_ref, twin_ref, mine, other, slots, sems):
    step = pl.program_id(0)

    def copies(mask):
        return weight_copies(
            narrow, layer, where_ref, mask, shard_ref, twin_ref, mine, other, slots.at[mask % 2], sems.at[mask % 2]
        )

    for mask in range(narrow):
        @pl.when(step == mask)
        def _():
            if mask == 0:
                for copy in copies(0):
                    copy.start()
            if mask + 1 < narrow:
                for copy in copies(mask + 1):
                    copy.start()
            for copy in copies(mask):
                copy.wait()
    return slots.at[lax.rem(step, 2)]


def weight_refs(refs, narrow):
    places, count = {}, 0
    for mask in range(narrow):
        for half in range(2):
            if mask & (mask - 1):
                places[mask, half] = refs[count]
                count += 1
            else:
                places[mask, half] = refs[count].at[half]
        if not mask & (mask - 1):
            count += 1
    twin = refs[count]
    return lambda mask, half: places[mask, half], lambda mask, half: twin.at[mask, half], refs[count + 1 :]


def mix_forward_body(narrow, layer, where_ref, low_ref, carry_ref, shift_a_ref, shift_g_ref, shard_ref, twin_ref, *rest):
    mine, other, (next_ref, low_next_ref, a_ref, g_ref, slots, sems) = weight_refs(rest, narrow)
    slot = weights_of_step(narrow, layer, where_ref, shard_ref, twin_ref, mine, other, slots, sems)
    low = low_ref[...]
    a = matmul(low, slot[0]) + shift_a_ref[...]
    g = matmul(low, slot[1]) + shift_g_ref[...]
    a_ref[...] = a
    g_ref[...] = g
    gate = jax.nn.sigmoid(g)
    following = gate * carry_ref[...] + (1.0 - gate) * gelu_curve(a)
    next_ref[...] = following
    low_next_ref[...] = following.astype(jnp.bfloat16)


def mix_forward(layer, where, low, carry, shift, shard, twin, mine, other):
    narrow = other.shape[0]
    words, filters = carry.shape
    part = filters // narrow
    flat = [*jax.tree.leaves(mine), other]
    block = pl.BlockSpec((words, part), lambda i, where: (0, where[0] ^ i))
    return pl.pallas_call(
        functools.partial(mix_forward_body, narrow, layer),
        grid_spec=pltpu.PrefetchScalarGridSpec(
            num_scalar_prefetch=1,
            grid=(narrow,),
            in_specs=[
                pl.BlockSpec((words, filters), lambda i, where: (0, 0)),
                block,
                pl.BlockSpec((1, part), lambda i, where: (0, where[0] ^ i)),
                pl.BlockSpec((1, part), lambda i, where: (0, narrow + (where[0] ^ i))),
            ]
            + [pl.BlockSpec(memory_space=pl.ANY)] * (2 + len(flat)),
            out_specs=[block] * 4,
            scratch_shapes=[
                pltpu.VMEM((2, 2, filters, part), jnp.bfloat16),
                pltpu.SemaphoreType.DMA((2, 4 * (filters // shard.shape[1] // 2))),
            ],
        ),
        out_shape=[
            jax.ShapeDtypeStruct((words, filters), kind) for kind in (jnp.float32, jnp.bfloat16, jnp.float32, jnp.float32)
        ],
        compiler_params=pltpu.CompilerParams(vmem_limit_bytes=48 << 20),
        cost_estimate=pl.CostEstimate(
            flops=words * filters * filters, bytes_accessed=filters * filters,
            transcendentals=0,
        ),
        name="mix_forward",
    )(where, low, carry, shift, shift, shard, twin, *flat)


def mix_backward_body(narrow, layer, where_ref, low_ref, carry_ref, a_ref, g_ref, pull_ref, shard_ref, twin_ref, *rest):
    mine, other, (own_ref, oth_ref, shift_ref, back_ref, slots, low_t_ref, sems) = weight_refs(rest, narrow)
    slot = weights_of_step(narrow, layer, where_ref, shard_ref, twin_ref, mine, other, slots, sems)

    @pl.when(pl.program_id(0) == 0)
    def _():
        for start in range(0, low_ref.shape[1], 256):
            low_t_ref[start : start + 256, :] = low_ref[:, start : start + 256].T

    a = a_ref[...]
    gate = jax.nn.sigmoid(g_ref[...])
    pull = pull_ref[...]
    pull_a = ((1.0 - gate) * gelu_slope(a) * pull).astype(jnp.bfloat16)
    pull_g = (gate * (1.0 - gate) * (carry_ref[...] - gelu_curve(a)) * pull).astype(jnp.bfloat16)
    half_rows = own_ref.shape[2]
    rows = shard_ref.shape[1]
    for half, grad in enumerate((pull_a, pull_g)):
        shift_ref[half, :, :] = jnp.sum(grad.astype(jnp.float32), axis=0, keepdims=True)
        for side, out_ref in enumerate((own_ref, oth_ref)):
            for chip in range(half_rows // rows):
                start = pl.multiple_of((2 * chip + (where_ref[2] ^ side)) * rows, rows)
                out_ref[0, half, chip * rows : (chip + 1) * rows, :] = matmul(
                    low_t_ref[pl.ds(start, rows), :], grad
                ).astype(jnp.bfloat16)
    back = matmul(pull_a, slot[0], CONTRACT_COLS) + matmul(pull_g, slot[1], CONTRACT_COLS)

    @pl.when(pl.program_id(0) == 0)
    def _():
        back_ref[...] = back

    @pl.when(pl.program_id(0) > 0)
    def _():
        back_ref[...] += back

    part = gate.shape[1]
    column = pl.multiple_of((where_ref[0] ^ pl.program_id(0)) * part, part)
    back_ref[:, pl.ds(column, part)] += gate * pull


def mix_backward(layer, where, low, carry, a, g, pull, shard, twin, mine, other):
    narrow = other.shape[0]
    words, filters = carry.shape
    part = filters // narrow
    flat = [*jax.tree.leaves(mine), other]
    block = pl.BlockSpec((words, part), lambda i, where: (0, where[0] ^ i))
    grad_block = pl.BlockSpec((1, 2, filters // 2, part), lambda i, where: (i, 0, 0, 0))
    grad_shape = jax.ShapeDtypeStruct((narrow, 2, filters // 2, part), jnp.bfloat16)
    return pl.pallas_call(
        functools.partial(mix_backward_body, narrow, layer),
        grid_spec=pltpu.PrefetchScalarGridSpec(
            num_scalar_prefetch=1,
            grid=(narrow,),
            in_specs=[pl.BlockSpec((words, filters), lambda i, where: (0, 0))]
            + [block] * 4
            + [pl.BlockSpec(memory_space=pl.ANY)] * (2 + len(flat)),
            out_specs=[
                grad_block,
                grad_block,
                pl.BlockSpec((2, 1, part), lambda i, where: (0, 0, where[0] ^ i)),
                pl.BlockSpec((words, filters), lambda i, where: (0, 0)),
            ],
            scratch_shapes=[
                pltpu.VMEM((2, 2, filters, part), jnp.bfloat16),
                pltpu.VMEM((filters, words), jnp.bfloat16),
                pltpu.SemaphoreType.DMA((2, 4 * (filters // shard.shape[1] // 2))),
            ],
        ),
        out_shape=[
            grad_shape,
            grad_shape,
            jax.ShapeDtypeStruct((2, 1, filters), jnp.float32),
            jax.ShapeDtypeStruct((words, filters), jnp.float32),
        ],
        compiler_params=pltpu.CompilerParams(vmem_limit_bytes=56 << 20),
        cost_estimate=pl.CostEstimate(
            flops=words * filters * filters, bytes_accessed=filters * filters,
            transcendentals=0,
        ),
        name="mix_backward",
    )(where, low, carry, a, g, pull, shard, twin, *flat)


def as_rows(value, lanes):
    count, size = value.shape
    lines = -(-size // lanes)
    return jnp.pad(value, ((0, 0), (0, lines * lanes - size))).reshape(count * lines, lanes)


def from_rows(rows, count, size):
    wide, lines, lanes = rows.shape
    value = rows.reshape(wide, count, lines // count * lanes)[:, :, :size]
    return value.transpose(1, 0, 2).reshape(count, wide * size)


def to_rows(value, wide, lanes):
    count, columns = value.shape
    size = columns // wide
    lines = -(-size // lanes)
    value = value.reshape(count, wide, size).transpose(1, 0, 2)
    return jnp.pad(value, ((0, 0), (0, 0), (0, lines * lanes - size))).reshape(wide, count * lines, lanes)


def split_rows(rows, sizes):
    pieces, start = [], 0
    for size in sizes:
        pieces.append(rows[..., start : start + size, :])
        start += size
    return pieces


def shards(
    narrow,
    wide,
    lengths,
    char_ids,
    char_counts,
    token_types,
    out_grad,
    char_table,
    conv_1,
    conv_2,
    conv_3,
    conv_4,
    conv_5,
    conv_6,
    conv_7,
    conv_bias,
    highway_weight,
    highway_bias,
    projection,
    position_table,
    type_table,
    embed_gain,
    embed_biases,
    qkv_weight,
    out_weight,
    ff_in,
    ff_in_bias,
    ff_out,
    layer_gains,
    layer_biases,
):
    convs = (conv_1, conv_2, conv_3, conv_4, conv_5, conv_6, conv_7)
    index = lax.axis_index("wide")
    place = lax.axis_index("narrow")
    where = jnp.stack([place, index // 2, index % 2]).astype(jnp.int32)
    lanes = conv_bias.shape[0]
    filters = lanes * wide
    model_width = embed_gain.shape[0] * wide
    vocab = char_table.shape[0] * wide // CDIM

    conv_block = jnp.concatenate([jnp.pad(k, ((0, TAP - k.shape[0]), (0, 0))) for k in convs], axis=1)
    model_rows = jnp.concatenate([type_table, embed_gain[None], embed_biases, layer_gains, layer_biases], axis=0)
    small = [
        conv_block,
        conv_bias[None],
        as_rows(highway_bias, lanes),
        as_rows(model_rows, lanes),
        as_rows(ff_in_bias[None], lanes),
        as_rows(char_table[None], lanes),
    ]
    small_sizes = [piece.shape[0] for piece in small]
    padding = -sum(small_sizes) % 16
    small_block = jnp.concatenate(small + [jnp.zeros((padding, lanes), jnp.bfloat16)], axis=0)
    everyone = lax.all_gather(small_block, "wide", axis=0, tiled=False)

    conv_rows, bias_rows, mix_rows, model_rows, inner_rows, table_rows = split_rows(everyone, small_sizes)
    top, start = [], 0
    for kernel in convs:
        size = kernel.shape[1]
        top.append(conv_rows[:, :, start : start + size].transpose(1, 0, 2).reshape(TAP, wide * size))
        start += size
    channels = [kernel.shape[1] * wide for kernel in convs]
    width_of = jnp.concatenate([jnp.full((1, count), k + 1, jnp.int32) for k, count in enumerate(channels)], axis=1)
    mask_rows = (width_of == lax.broadcasted_iota(jnp.int32, (KROWS - TAP - 1, 1), 0) + 1).astype(jnp.bfloat16)
    kern = jnp.concatenate([jnp.concatenate(top, axis=1), from_rows(bias_rows, 1, lanes), mask_rows], axis=0)
    highway_shift = from_rows(mix_rows, 2, highway_bias.shape[1]).astype(jnp.float32)
    vectors = from_rows(model_rows, 13, embed_gain.shape[0]).astype(jnp.float32)
    type_vectors, embed_gain_full, embed_shift = vectors[0:2], vectors[2], vectors[3:5]
    gain_rows, shift_rows = vectors[5:7], vectors[7:13]
    inner_shift = from_rows(inner_rows, 1, ff_in_bias.shape[0])[0].astype(jnp.float32)
    table = from_rows(table_rows, 1, char_table.shape[0]).reshape(vocab, CDIM)

    seq_count, seq_len, char_slots = char_ids.shape
    word_count = seq_count * seq_len
    counts = char_counts.reshape(word_count, 1)
    slots = lax.broadcasted_iota(jnp.int32, (1, char_slots), 1)
    ids = jnp.where(slots < counts, char_ids.reshape(word_count, char_slots), -1)
    row_keep = (
        (lax.broadcasted_iota(jnp.int32, (seq_count, seq_len), 1) < lengths[:, None])
        .astype(jnp.float32)
        .reshape(word_count, 1)
    )
    type_one = (token_types.reshape(word_count, 1) == 1).astype(jnp.float32)

    levels = levels_of(narrow)
    tables = table_turns(table)
    blocks = word_count // CONV_BLOCK

    def stacked_rows(pieces):
        value = jnp.concatenate(pieces, axis=0)
        return jnp.pad(value, ((0, -value.shape[0] % 16), (0, 0)))

    def side_by_side(value):
        return [value[:, i : i + model_width] for i in range(0, value.shape[1], model_width)]

    deep_one = stacked_rows([projection, position_table] + side_by_side(qkv_weight) + [out_weight])
    deep_two = stacked_rows(side_by_side(ff_in) + [ff_out])
    kern, mix_shards, deep_one, deep_two = tie(kern, highway_weight, deep_one, deep_two)
    chips = wide // 2
    stacks = [gather_chips(own_columns(mix_shards[number], place, narrow), wide) for number in range(2)]
    state = []
    for call in range(blocks):
        state = conv_forward(call, ids, counts, tables, kern, state)
    stacks[0], state, deep_one = tie(stacks[0], state, deep_one)
    known = [{0: other_chips(stacks[0], index // 2)}, None]
    spread_level(known[0], narrow, 1)
    windows, totals = state
    places = (jnp.maximum(counts - width_of, 0) + 1).astype(jnp.float32)
    pooled = jnp.log(totals / places)
    carried = gelu_curve(pooled)
    low_state = carried.astype(jnp.bfloat16)
    known[0], stacks[1], mix_shards, low_state, deep_one, deep_two = tie(
        known[0], stacks[1], mix_shards, low_state, deep_one, deep_two
    )
    for level in levels[1:]:
        spread_level(known[0], narrow, level)
    twin = core_swap(mix_shards, wide)
    full_one = lax.all_gather(deep_one, "wide", axis=0, tiled=False)
    full_two = lax.all_gather(deep_two, "wide", axis=0, tiled=False)
    known[0], twin, stacks[1] = tie(known[0], twin, stacks[1])
    other = swap_known(known[0], narrow, wide)
    known[1] = {0: other_chips(stacks[1], index // 2)}
    spread_level(known[1], narrow, 1)
    states, low_states, mixes, mixers = [], [], [], []

    def mix(number, carried, low_state, other):
        mine = [known[number][mask] for mask in range(narrow)]
        mixers.append((mine, other))
        low_states.append(low_state)
        states.append(carried)
        carried, low_state, mix_a, mix_g = mix_forward(
            number, where, low_state, carried, highway_shift[number][None], highway_weight, twin, mine, other
        )
        mixes.append((mix_a, mix_g))
        return carried, low_state

    carried, low_state = mix(0, carried, low_state, other)
    known[1], carried, low_state = tie(known[1], carried, low_state)
    for level in levels[1:]:
        spread_level(known[1], narrow, level)
    known[1], low_state = tie(known[1], low_state)
    carried, low_top = mix(1, carried, low_state, swap_known(known[1], narrow, wide))
    full_one, low_top = tie(full_one, low_top)

    def taken(full, sizes):
        pieces, start = [], 0
        for size in sizes:
            pieces.append(full[:, start : start + size].reshape(wide * size, model_width))
            start += size
        return pieces

    deep_rows = qkv_weight.shape[0]
    projection_full, position_full, *qkv_parts, out_full = taken(
        full_one, [projection.shape[0], position_table.shape[0]] + [deep_rows] * 4
    )
    qkv_full = jnp.concatenate(qkv_parts, axis=1)
    position_rows = jnp.tile(position_full.astype(jnp.float32), (seq_count, 1))
    embed_sum = (
        matmul(low_top, projection_full)
        + embed_shift[0]
        + position_rows
        + type_vectors[0] * (1.0 - type_one)
        + type_vectors[1] * type_one
    )
    embedded = normalize(embed_sum, embed_gain_full, embed_shift[1])
    low_in = embedded.astype(jnp.bfloat16)
    bias_full = jnp.concatenate([shift_rows[0], jnp.zeros_like(shift_rows[0]), shift_rows[1]])
    projected = (matmul(low_in, qkv_full) + bias_full).astype(jnp.bfloat16)
    proj_seqs = projected.reshape(seq_count, seq_len, -1)
    context_seqs, log_totals = lax.map(lambda seq_pair: attend(seq_pair[0], seq_pair[1]), (proj_seqs, lengths))
    context = context_seqs.reshape(word_count, -1)
    full_two, context = tie(full_two, context)
    position_rows = jnp.tile(position_full.astype(jnp.float32), (seq_count, 1))
    embed_sum = (
        matmul(low_top, projection_full)
        + embed_shift[0]
        + position_rows
        + type_vectors[0] * (1.0 - type_one)
        + type_vectors[1] * type_one
    )
    embedded = normalize(embed_sum, embed_gain_full, embed_shift[1])
    low_in = embedded.astype(jnp.bfloat16)
    bias_full = jnp.concatenate([shift_rows[0], jnp.zeros_like(shift_rows[0]), shift_rows[1]])
    projected = (matmul(low_in, qkv_full) + bias_full).astype(jnp.bfloat16)
    proj_seqs = projected.reshape(seq_count, seq_len, -1)
    context_seqs, log_totals = lax.map(lambda seq_pair: attend(seq_pair[0], seq_pair[1]), (proj_seqs, lengths))
    context = context_seqs.reshape(word_count, -1)
    full_two, context = tie(full_two, context)
    *inner_parts, ff_out_full = taken(full_two, [deep_rows] * (ff_in.shape[1] // model_width) + [ff_out.shape[0]])
    ff_in_full = jnp.concatenate(inner_parts, axis=1)
    first_in = embedded + matmul(context, out_full) + shift_rows[2]
    first_out = normalize(first_in, gain_rows[0], shift_rows[3])
    low_first = first_out.astype(jnp.bfloat16)
    inner_pre = matmul(low_first, ff_in_full) + inner_shift
    activated = gelu_curve(inner_pre).astype(jnp.bfloat16)
    second_in = first_out + matmul(activated, ff_out_full) + shift_rows[4]
    final_out = normalize(second_in, gain_rows[1], shift_rows[5])
    hidden_out = (final_out * row_keep).reshape(seq_count, seq_len, -1)

    grad_top = out_grad.reshape(word_count, -1).astype(jnp.float32) * row_keep
    norm_pull = jax.vjp(normalize, second_in, gain_rows[1], shift_rows[5])[1]
    grad_second, grad_gain_two, grad_shift_five = norm_pull(grad_top)
    grad_ffn = grad_second.astype(jnp.bfloat16)
    grad_shift_four = jnp.sum(grad_ffn, axis=0, dtype=jnp.float32)
    weight_ff_out = matmul(activated, grad_ffn, CONTRACT_ROWS)
    grad_inner = (matmul(grad_ffn, ff_out_full, CONTRACT_COLS) * gelu_slope(inner_pre)).astype(jnp.bfloat16)
    grad_ff_bias = jnp.sum(grad_inner, axis=0, dtype=jnp.float32)
    weight_ff_in = matmul(low_first, grad_inner, CONTRACT_ROWS)
    grad_first = grad_second + matmul(grad_inner, ff_in_full, CONTRACT_COLS)
    norm_pull = jax.vjp(normalize, first_in, gain_rows[0], shift_rows[3])[1]
    grad_res, grad_gain_one, grad_shift_three = norm_pull(grad_first)
    grad_attn = grad_res.astype(jnp.bfloat16)
    grad_shift_two = jnp.sum(grad_attn, axis=0, dtype=jnp.float32)
    weight_out = matmul(context, grad_attn, CONTRACT_ROWS)
    grad_context = matmul(grad_attn, out_full, CONTRACT_COLS).astype(jnp.bfloat16)
    grad_seqs = lax.map(
        lambda seq_quad: attend_back(seq_quad[0], seq_quad[1], seq_quad[2], seq_quad[3]),
        (proj_seqs, log_totals, grad_context.reshape(seq_count, seq_len, -1), lengths),
    )
    grad_proj = grad_seqs.reshape(word_count, -1)
    grad_shift_zero = jnp.sum(grad_proj[:, :model_width], axis=0, dtype=jnp.float32)
    grad_shift_one = jnp.sum(grad_proj[:, 2 * model_width :], axis=0, dtype=jnp.float32)
    weight_qkv = matmul(low_in, grad_proj, CONTRACT_ROWS)
    grad_embedded = grad_res + matmul(grad_proj, qkv_full, CONTRACT_COLS)
    norm_pull = jax.vjp(normalize, embed_sum, embed_gain_full, embed_shift[1])[1]
    grad_sum, grad_embed_gain, grad_embed_shift = norm_pull(grad_embedded)
    grad_embed = grad_sum.astype(jnp.bfloat16)
    grad_embed_zero = jnp.sum(grad_embed, axis=0, dtype=jnp.float32)
    grad_position = jnp.sum(grad_embed.reshape(seq_count, seq_len, -1), axis=0, dtype=jnp.float32)
    type_mask = type_one.astype(jnp.bfloat16)
    grad_type_one = jnp.sum(grad_embed * type_mask, axis=0, dtype=jnp.float32)
    grad_type_zero = jnp.sum(grad_embed * (1 - type_mask), axis=0, dtype=jnp.float32)
    weight_proj = matmul(low_top, grad_embed, CONTRACT_ROWS)
    grad_carry = matmul(grad_embed, projection_full, CONTRACT_COLS)

    def deep(value):
        rows = value.shape[0] // wide
        value = value.astype(jnp.bfloat16).reshape(wide, rows, value.shape[1])
        return [value[:, :, i : i + model_width] for i in range(0, value.shape[2], model_width)]

    def reduce_wide(values):
        parts = [deep(value) for value in values]
        total = lax.psum_scatter(jnp.concatenate([p for part in parts for p in part], axis=1), "wide", scatter_dimension=0)
        return total, [[p.shape[1] for p in part] for part in parts]

    def split_deep(total, sizes):
        values, start = [], 0
        for part in sizes:
            pieces = []
            for size in part:
                pieces.append(total[start : start + size])
                start += size
            values.append(jnp.concatenate(pieces, axis=1).astype(jnp.float32))
        return values

    first_sum, first_sizes = reduce_wide([weight_ff_out, weight_ff_in])

    shift_high, weight_high = [None, None], [None, None]

    def unmix(number, pull):
        mix_a, mix_g = mixes[number]
        own_part, other_part, shift_grad, back = mix_backward(
            number, where, low_states[number], states[number], mix_a, mix_g, pull, highway_weight, twin, *mixers[number]
        )
        shift_high[number] = shift_grad.reshape(2 * filters)
        return own_part, other_part, back


    def begun(own_part, got):
        return [(own_part[:, half], got[:, half]) for half in range(2)]

    def send_home(terms):
        blocks = [add_low(parts[0], arrived[0]).reshape(chips, -1, parts.shape[-1]) for parts, arrived in terms]
        return lax.psum_scatter(
            jnp.stack(blocks, axis=1), "wide", scatter_dimension=0, axis_index_groups=chip_groups(wide)
        )

    def laid_out(totals):
        pieces = []
        for half in range(2):
            table = jnp.stack([totals[mask][half] for mask in range(narrow)])
            for block in range(narrow):
                pieces.append(lax.dynamic_index_in_dim(table, place ^ block, 0, keepdims=False))
        return jnp.concatenate(pieces, axis=1).astype(jnp.float32)

    def convolve_back(first, last, state):
        for call in range(first, last):
            state = conv_backward(call, ids.T, windows, scaled, kern, state)
        return state

    rounds = range(narrow.bit_length() - 1)
    rounds = range(narrow.bit_length() - 1)
    own_one, other_one, pull = unmix(1, grad_carry)
    got_one = core_swap(other_one, wide)
    second_parts = [weight_out.astype(jnp.bfloat16), weight_qkv.astype(jnp.bfloat16), weight_proj.astype(jnp.bfloat16)]
    got_one, second_parts, pull = tie(got_one, second_parts, pull)
    second_sum, second_sizes = reduce_wide(second_parts + [grad_position])
    terms_one = collect_round(begun(own_one, got_one), narrow, 0)
    staying = [parts for parts, _ in terms_one]
    staying, pull = tie(staying, pull)
    own_zero, other_zero, pull = unmix(0, pull)
    terms_one, own_zero, other_zero, pull = tie(
        [(parts, sent) for parts, (_, sent) in zip(staying, terms_one)], own_zero, other_zero, pull
    )
    got_zero = core_swap(other_zero, wide)
    for turn in rounds[1:]:
        terms_one = collect_round(terms_one, narrow, turn)
    scaled = pull * gelu_slope(pooled) / totals
    terms_one, got_zero, scaled = tie(terms_one, got_zero, scaled)
    home_one = send_home(terms_one)
    terms_zero = collect_round(begun(own_zero, got_zero), narrow, 0)
    state = [jnp.zeros(kern.shape, jnp.float32), jnp.zeros((VROWS, 128), jnp.float32)]
    state = convolve_back(0, blocks // 2, state)
    state, terms_zero = tie(state, terms_zero)
    for turn in rounds[1:]:
        terms_zero = collect_round(terms_zero, narrow, turn)
    state = convolve_back(blocks // 2, blocks * 3 // 4, state)
    state, terms_zero, first_sum, second_sum = tie(state, terms_zero, first_sum, second_sum)
    home_zero = send_home(terms_zero)
    deep_sum = jnp.concatenate([first_sum, second_sum], axis=0)
    deep_half = deep_sum.shape[0] // 2

    def swap_axis(value, turn):
        return [
            hop(value[half * deep_half : (half + 1) * deep_half], narrow, bits_of(narrow, half)[turn]) for half in range(2)
        ]

    def add_swapped(value, arrived):
        return add_low(value, jnp.concatenate(arrived, axis=0))

    arrived = swap_axis(deep_sum, 0)
    state = convolve_back(blocks * 3 // 4, blocks, state)
    state, home_one, deep_sum, arrived = tie(state, home_one, deep_sum, arrived)
    total_one = {0: home_one}
    spread_level(total_one, narrow, 1)
    deep_sum = add_swapped(deep_sum, arrived)
    arrived = swap_axis(deep_sum, 1)
    kern_grad, table_grad = state
    table_grad = table_grad[:vocab].reshape(vocab, 8, CDIM).sum(axis=1)
    conv_rows, start = [], 0
    for count in channels:
        part = kern_grad[:TAP, start : start + count].reshape(TAP, wide, count // wide)
        conv_rows.append(part.transpose(1, 0, 2))
        start += count
    model_grads = jnp.stack(
        [
            grad_type_zero,
            grad_type_one,
            grad_embed_gain,
            grad_embed_zero,
            grad_embed_shift,
            grad_gain_one,
            grad_gain_two,
            grad_shift_zero,
            grad_shift_one,
            grad_shift_two,
            grad_shift_three,
            grad_shift_four,
            grad_shift_five,
        ]
    )
    small = [
        jnp.concatenate(conv_rows, axis=2),
        to_rows(kern_grad[TAP : TAP + 1], wide, lanes),
        to_rows(jnp.stack(shift_high), wide, lanes),
        to_rows(model_grads, wide, lanes),
        to_rows(grad_ff_bias[None], wide, lanes),
        to_rows(table_grad.reshape(1, -1), wide, lanes),
        jnp.zeros((wide, padding, lanes), jnp.float32),
    ]
    small_part = jnp.concatenate(small, axis=1).astype(jnp.bfloat16).reshape(chips, 2, -1, lanes)

    def exchange(value, at, bit):
        side = (index // bit) % 2
        got = lax.ppermute(
            lax.dynamic_index_in_dim(value, 1 - side, at, keepdims=False), "wide", [(i, i ^ bit) for i in range(wide)]
        )
        return lax.dynamic_index_in_dim(value, side, at, keepdims=False), got

    kept, got = exchange(small_part, 1, 1)
    got, total_one, home_zero, deep_sum, arrived = tie(got, total_one, home_zero, deep_sum, arrived)
    deep_sum = add_swapped(deep_sum, arrived)
    for turn in rounds[2:]:
        deep_sum = add_swapped(deep_sum, swap_axis(deep_sum, turn))
    total_zero = {0: home_zero}
    spread_level(total_zero, narrow, 1)
    for level in levels[1:]:
        spread_level(total_one, narrow, level)
    small_sum = add_low(kept, got)
    bit = wide // 2
    while bit > 1:
        kept, got = exchange(small_sum.reshape(2, -1, *small_sum.shape[1:]), 0, bit)
        small_sum = add_low(kept, got)
        bit //= 2
    total_zero, small_sum = tie(total_zero, small_sum)
    for level in levels[1:]:
        spread_level(total_zero, narrow, level)
    small_sum = small_sum[0].astype(jnp.float32)
    for bit in bits_of(narrow, 0):
        small_sum = small_sum + hop(small_sum.astype(jnp.bfloat16), narrow, bit).astype(jnp.float32)
    weight_high = [laid_out(total_zero), laid_out(total_one)]
    grad_ff_out_sum, grad_ff_in_sum = split_deep(deep_sum[: first_sum.shape[0]], first_sizes)
    grad_out_sum, grad_qkv_sum, grad_projection_sum, grad_position_sum = split_deep(
        deep_sum[first_sum.shape[0] :], second_sizes
    )
    conv_sum, bias_sum, mix_sum, model_sum, inner_sum, table_sum = split_rows(small_sum, small_sizes)
    conv_grads, start = [], 0
    for kernel in convs:
        conv_grads.append(conv_sum[: kernel.shape[0], start : start + kernel.shape[1]])
        start += kernel.shape[1]
    mix_sum = from_rows(mix_sum[None], 2, highway_bias.shape[1])
    model_sum = from_rows(model_sum[None], 13, embed_gain.shape[0])
    return (
        hidden_out,
        from_rows(table_sum[None], 1, char_table.shape[0])[0],
        *conv_grads,
        bias_sum[0],
        jnp.stack(weight_high),
        mix_sum,
        grad_projection_sum,
        grad_position_sum,
        model_sum[0:2],
        model_sum[2],
        model_sum[3:5],
        grad_qkv_sum,
        grad_out_sum,
        grad_ff_in_sum,
        from_rows(inner_sum[None], 1, ff_in_bias.shape[0])[0],
        grad_ff_out_sum,
        model_sum[5:7],
        model_sum[7:13],
    )


def solution(mesh):
    in_specs = (
        P(("narrow", "wide")),
        P(("narrow", "wide"), None, None),
        P(("narrow", "wide"), None),
        P(("narrow", "wide"), None),
        P(("narrow", "wide"), None, None),
        P("wide"),
        P(None, "wide"),
        P(None, "wide"),
        P(None, "wide"),
        P(None, "wide"),
        P(None, "wide"),
        P(None, "wide"),
        P(None, "wide"),
        P("wide"),
        P(None, "wide", None),
        P(None, "wide"),
        P("wide", None),
        P("wide", None),
        P(None, "wide"),
        P("wide"),
        P(None, "wide"),
        P("wide", None),
        P("wide", None),
        P("wide", None),
        P("wide"),
        P("wide", None),
        P(None, "wide"),
        P(None, "wide"),
    )
    out_specs = (
        P(("narrow", "wide"), None, None),
        P("wide"),
        P(None, "wide"),
        P(None, "wide"),
        P(None, "wide"),
        P(None, "wide"),
        P(None, "wide"),
        P(None, "wide"),
        P(None, "wide"),
        P("wide"),
        P(None, "wide", None),
        P(None, "wide"),
        P("wide", None),
        P("wide", None),
        P(None, "wide"),
        P("wide"),
        P(None, "wide"),
        P("wide", None),
        P("wide", None),
        P("wide", None),
        P("wide"),
        P("wide", None),
        P(None, "wide"),
        P(None, "wide"),
    )
    run = functools.partial(shards, mesh.shape["narrow"], mesh.shape["wide"])
    return jax.shard_map(run, mesh=mesh, in_specs=in_specs, out_specs=out_specs, check_vma=False)
```

```python
import functools
import math

import jax
import jax.numpy as jnp
from jax import lax
from jax.experimental import pallas as pl
from jax.experimental.pallas import tpu as pltpu
from jax.sharding import PartitionSpec as P

HDIM = 64
CDIM = 16
WCH = 50
TAP = 112
KROWS = 128
MASK_LOW = -1e30
VPAD = 384
VROWS = 272
FLAT = 896
CONV_BLOCK = 128

EPSILON = 1e-06
MASKED_SCORE = -1e30
ROOT_HALF = 0.7071067811865476
NORMAL_PEAK = 0.3989422804014327
CONTRACT_ROWS = (((0,), (0,)), ((), ()))
CONTRACT_COLS = (((1,), (1,)), ((), ()))
INNER_FIRST = (((1,), (0,)), ((), ()))


def gelu_curve(value):
    return 0.5 * value * (1.0 + lax.erf(value * ROOT_HALF))


def gelu_slope(value):
    return 0.5 * (1.0 + lax.erf(value * ROOT_HALF)) + value * NORMAL_PEAK * jnp.exp(
        -0.5 * value * value
    )


def normalize(value, gain, shift):
    average = jnp.mean(value, axis=-1, keepdims=True)
    centred = value - average
    spread = jnp.mean(centred * centred, axis=-1, keepdims=True)
    return centred * lax.rsqrt(spread + EPSILON) * gain + shift


def matmul(left, right, dims=INNER_FIRST):
    return lax.dot_general(left, right, dims, preferred_element_type=jnp.float32)


def conv_fwd_body(block, filters, held, ids_ref, cnt_ref, table_ref, kern_ref, *rest):
    x_ref, den_ref, flat, hot = rest[held:]
    lane = lax.broadcasted_iota(jnp.int32, (block, VPAD), 1)
    groups = FLAT // 128
    for turn in range(8):
        for g in range(groups):
            slot = 8 * g + turn
            if slot < WCH:
                col = ids_ref[:, slot:slot + 1]
                hot[g * block:(g + 1) * block, :] = (col == lane).astype(jnp.float32).astype(jnp.bfloat16)
            else:
                hot[g * block:(g + 1) * block, :] = jnp.zeros((block, VPAD), jnp.bfloat16)
        found = matmul(hot[...], table_ref[turn])
        for g in range(groups):
            part = found[g * block:(g + 1) * block, :]
            if turn == 0:
                flat[:, g * 128:(g + 1) * 128] = part
            else:
                flat[:, g * 128:(g + 1) * 128] += part
    flat[:, FLAT:] = jnp.zeros((block, 128), jnp.float32)
    lane_x = lax.broadcasted_iota(jnp.int32, (block, KROWS), 1)
    width = lane_x - TAP
    count = jnp.broadcast_to(cnt_ref[...], (block, KROWS))
    reach = jnp.maximum(count, width)
    for place in range(WCH):
        a, r = divmod(place, 8)
        first = flat[:, a * 128:(a + 1) * 128]
        if r:
            second = flat[:, (a + 1) * 128:(a + 2) * 128]
            first = pltpu.roll(first, 128 - 16 * r, 1)
            second = pltpu.roll(second, 128 - 16 * r, 1)
            first = jnp.where(lane_x < 128 - 16 * r, first, second)
        extra = jnp.where(width == 0, 1.0, jnp.where((width <= 7) & (place + width > reach), MASK_LOW, 0.0))
        x_ref[place * block:(place + 1) * block, :] = jnp.where(width < 0, first, extra).astype(jnp.bfloat16)

    step = 4
    den_ref[...] = jnp.zeros_like(den_ref)
    tile = 512

    def piece(start, count_p, lo, hi):
        rows = x_ref[pl.ds(start, count_p * block), :]
        summed = matmul(rows, kern_ref[:, lo:hi])
        e = jnp.exp(summed)
        total = e[:block]
        for i in range(1, count_p):
            total = total + e[i * block:(i + 1) * block]
        den_ref[:, lo:hi] += total

    def chunk(i, carry):
        start = pl.multiple_of(i * step * block, step * block)
        for lo in range(0, filters, tile):
            piece(start, step, lo, lo + tile)
        return carry

    lax.fori_loop(0, 11, chunk, 0)
    for lo in range(0, 1024, tile):
        piece(44 * block, 4, lo, lo + tile)
    piece(48 * block, 2, 0, 256)


def conv_forward(call, count, ids, counts, tables, kern, state):
    block = CONV_BLOCK
    words, filters = ids.shape[0], kern.shape[1]
    return pl.pallas_call(
        functools.partial(conv_fwd_body, block, filters, len(state)),
        grid=(count,),
        in_specs=[
            pl.BlockSpec((block, ids.shape[1]), lambda i: (call + i, 0)),
            pl.BlockSpec((block, 1), lambda i: (call + i, 0)),
            pl.BlockSpec(tables.shape, lambda i: (0, 0, 0)),
            pl.BlockSpec(kern.shape, lambda i: (0, 0)),
        ]
        + [pl.BlockSpec(memory_space=pl.ANY)] * len(state),
        out_specs=[
            pl.BlockSpec((WCH * block, KROWS), lambda i: (call + i, 0)),
            pl.BlockSpec((block, filters), lambda i: (call + i, 0)),
        ],
        out_shape=[
            jax.ShapeDtypeStruct((words * WCH, KROWS), jnp.bfloat16),
            jax.ShapeDtypeStruct((words, filters), jnp.float32),
        ],
        input_output_aliases={4: 0, 5: 1} if state else {},
        scratch_shapes=[
            pltpu.VMEM((block, FLAT + 128), jnp.float32),
            pltpu.VMEM((FLAT // 128 * block, VPAD), jnp.bfloat16),
        ],
        compiler_params=pltpu.CompilerParams(vmem_limit_bytes=40 << 20),
        cost_estimate=pl.CostEstimate(
            flops=count * block * WCH * 32 * filters,
            bytes_accessed=count * block * filters,
            transcendentals=0,
        ),
        name="conv_forward",
    )(ids, counts, tables, kern, *state)


def conv_bwd_body(block, filters, idst_ref, x_ref, ginv_ref, kern_ref, kern_in_ref, table_in_ref, kern_grad_ref, table_grad_ref, gx, flat, hot, part):
    @pl.when(pl.program_id(0) == 0)
    def _():
        kern_grad_ref[...] = kern_in_ref[...]
        table_grad_ref[...] = table_in_ref[...]


    tile = 512
    step = 4

    def piece(start, count_p, lo, hi):
        rows = x_ref[pl.ds(start, count_p * block), :]
        k = kern_ref[:, lo:hi]
        e = jnp.exp(matmul(rows, k))
        scale = ginv_ref[:, lo:hi]
        g = jnp.concatenate([e[i * block:(i + 1) * block] * scale for i in range(count_p)], axis=0).astype(jnp.bfloat16)
        kern_grad_ref[:, lo:hi] += matmul(rows, g, CONTRACT_ROWS)
        return matmul(g, k, CONTRACT_COLS)

    def chunk(i, carry):
        start = pl.multiple_of(i * step * block, step * block)
        total = piece(start, step, 0, tile)
        for lo in range(tile, filters, tile):
            total = total + piece(start, step, lo, lo + tile)
        gx[pl.ds(start, step * block), :] = total
        return carry

    lax.fori_loop(0, 11, chunk, 0)
    gx[44 * block:48 * block, :] = piece(44 * block, 4, 0, 512) + piece(44 * block, 4, 512, 1024)
    gx[48 * block:50 * block, :] = piece(48 * block, 2, 0, 256)

    flat[...] = jnp.zeros_like(flat)
    lane_x = lax.broadcasted_iota(jnp.int32, (block, 128), 1)
    for place in range(WCH):
        a, r = divmod(place, 8)
        value = jnp.where(lane_x < TAP, gx[place * block:(place + 1) * block, :], 0.0)
        if r:
            value = pltpu.roll(value, 16 * r, 1)
            flat[:, a * 128:(a + 1) * 128] += jnp.where(lane_x >= 16 * r, value, 0.0)
            flat[:, (a + 1) * 128:(a + 2) * 128] += jnp.where(lane_x < 16 * r, value, 0.0)
        else:
            flat[:, a * 128:(a + 1) * 128] += value
    groups = FLAT // 128
    for g in range(groups):
        part[g * block:(g + 1) * block, :] = flat[:, g * 128:(g + 1) * 128].astype(jnp.bfloat16)
    sub = lax.broadcasted_iota(jnp.int32, (VROWS, block), 0)
    lane_t = lax.broadcasted_iota(jnp.int32, (VROWS, 128), 1)
    for turn in range(8):
        for g in range(groups):
            slot = 8 * g + turn
            if slot < WCH:
                row = idst_ref[slot:slot + 1, :]
                hot[:, g * block:(g + 1) * block] = (row == sub).astype(jnp.float32).astype(jnp.bfloat16)
            else:
                hot[:, g * block:(g + 1) * block] = jnp.zeros((VROWS, block), jnp.bfloat16)
        found = matmul(hot[...], part[...])
        table_grad_ref[...] += jnp.where((lane_t >= 16 * turn) & (lane_t < 16 * turn + 16), found, 0.0)


def conv_backward(call, count, ids_t, x, ginv, kern, state):
    block = CONV_BLOCK
    filters = ginv.shape[1]
    whole = [pl.BlockSpec(kern.shape, lambda i: (0, 0)), pl.BlockSpec((VROWS, 128), lambda i: (0, 0))]
    return pl.pallas_call(
        functools.partial(conv_bwd_body, block, filters),
        grid=(count,),
        in_specs=[
            pl.BlockSpec((ids_t.shape[0], block), lambda i: (0, call + i)),
            pl.BlockSpec((WCH * block, KROWS), lambda i: (call + i, 0)),
            pl.BlockSpec((block, filters), lambda i: (call + i, 0)),
            pl.BlockSpec(kern.shape, lambda i: (0, 0)),
        ]
        + whole,
        out_specs=whole,
        out_shape=[
            jax.ShapeDtypeStruct(kern.shape, jnp.float32),
            jax.ShapeDtypeStruct((VROWS, 128), jnp.float32),
        ],
        input_output_aliases={4: 0, 5: 1},
        scratch_shapes=[
            pltpu.VMEM((WCH * block, 128), jnp.float32),
            pltpu.VMEM((block, FLAT + 128), jnp.float32),
            pltpu.VMEM((VROWS, FLAT // 128 * block), jnp.bfloat16),
            pltpu.VMEM((FLAT // 128 * block, 128), jnp.bfloat16),
        ],
        compiler_params=pltpu.CompilerParams(vmem_limit_bytes=60 << 20),
        cost_estimate=pl.CostEstimate(
            flops=count * block * WCH * 64 * filters,
            bytes_accessed=count * block * filters,
            transcendentals=0,
        ),
        name="conv_backward",
    )(ids_t, x, ginv, kern, *state)


def table_turns(table):
    padded = jnp.pad(table, ((0, VPAD - table.shape[0]), (0, 0)))
    return jnp.stack([jnp.pad(padded, ((0, 0), (16 * r, 112 - 16 * r))) for r in range(8)])


def head_scores(length_ref, q, k, head):
    words, width = q.shape
    lane = lax.broadcasted_iota(jnp.int32, (words, width), 1)
    inside = (lane >= head * HDIM) & (lane < (head + 1) * HDIM)
    own = jnp.where(inside, q.astype(jnp.float32), 0.0).astype(jnp.bfloat16)
    key = lax.broadcasted_iota(jnp.int32, (words, words), 0)
    scores = matmul(k, own, CONTRACT_COLS) * (1.0 / math.sqrt(HDIM))
    return own, inside, key < length_ref[0], scores


def attend_body(length_ref, q_ref, k_ref, v_ref, context_ref, total_ref):
    q, k, v = q_ref[...], k_ref[...], v_ref[...]
    words, width = q.shape
    row = lax.broadcasted_iota(jnp.int32, (width, words), 0)
    context = jnp.zeros((width, words), jnp.float32)
    for head in range(2):
        _, _, keep, scores = head_scores(length_ref, q, k, head)
        scores = jnp.where(keep, scores, MASKED_SCORE)
        highest = jnp.max(scores, axis=0, keepdims=True)
        exponent = jnp.exp(scores - highest)
        denominator = jnp.sum(exponent, axis=0, keepdims=True)
        weights = (exponent * (1.0 / denominator)).astype(jnp.bfloat16)
        own = matmul(v, weights, CONTRACT_ROWS)
        context = jnp.where(row >= head * HDIM, own, context)
        total_ref[0, head : head + 1, :] = highest + jnp.log(denominator)
    context_ref[...] = context.T.astype(jnp.bfloat16)


def attend_back_body(length_ref, q_ref, k_ref, v_ref, pull_ref, total_ref, grad_ref):
    q, k, v = q_ref[...], k_ref[...], v_ref[...]
    pull = pull_ref[...].astype(jnp.float32)
    words, width = q.shape
    row = lax.broadcasted_iota(jnp.int32, (width, words), 0)
    scale = 1.0 / math.sqrt(HDIM)
    grad_q = jnp.zeros((width, words), jnp.float32)
    grad_k = jnp.zeros((words, width), jnp.float32)
    grad_v = jnp.zeros((words, width), jnp.float32)
    for head in range(2):
        own, inside, keep, scores = head_scores(length_ref, q, k, head)
        weights = jnp.where(keep, jnp.exp(scores - total_ref[0, head : head + 1, :]), 0.0)
        own_pull = jnp.where(inside, pull, 0.0).astype(jnp.bfloat16)
        grad_weights = matmul(v, own_pull, CONTRACT_COLS)
        dots = jnp.sum(weights * grad_weights, axis=0, keepdims=True)
        grad_scores = (weights * (grad_weights - dots)).astype(jnp.bfloat16)
        grad_v = grad_v + matmul(weights.astype(jnp.bfloat16), own_pull)
        grad_k = grad_k + matmul(grad_scores, own)
        grad_q = jnp.where(row >= head * HDIM, matmul(k, grad_scores, CONTRACT_ROWS), grad_q)
    grad_ref[0] = (grad_q.T * scale).astype(jnp.bfloat16)
    grad_ref[1] = (grad_k * scale).astype(jnp.bfloat16)
    grad_ref[2] = grad_v.astype(jnp.bfloat16)


def attention_specs(words, columns):
    return pl.BlockSpec((words, 2 * HDIM), lambda i, length: (0, i)), columns // (2 * HDIM)


def attend(length, q, k, v):
    words, columns = q.shape
    block, pairs = attention_specs(words, columns)
    return pl.pallas_call(
        attend_body,
        grid_spec=pltpu.PrefetchScalarGridSpec(
            num_scalar_prefetch=1,
            grid=(pairs,),
            in_specs=[block] * 3,
            out_specs=[block, pl.BlockSpec((1, 8, words), lambda i, length: (i, 0, 0))],
        ),
        out_shape=[
            jax.ShapeDtypeStruct((words, columns), jnp.bfloat16),
            jax.ShapeDtypeStruct((pairs, 8, words), jnp.float32),
        ],
        compiler_params=pltpu.CompilerParams(vmem_limit_bytes=40 << 20),
        cost_estimate=pl.CostEstimate(flops=words * words * columns, bytes_accessed=words * columns, transcendentals=0),
        name="attend",
    )(length, q, k, v)


def attend_back(length, q, k, v, pull, totals):
    words, columns = q.shape
    block, pairs = attention_specs(words, columns)
    return pl.pallas_call(
        attend_back_body,
        grid_spec=pltpu.PrefetchScalarGridSpec(
            num_scalar_prefetch=1,
            grid=(pairs,),
            in_specs=[block] * 4 + [pl.BlockSpec((1, 8, words), lambda i, length: (i, 0, 0))],
            out_specs=pl.BlockSpec((3, words, 2 * HDIM), lambda i, length: (0, 0, i)),
        ),
        out_shape=jax.ShapeDtypeStruct((3, words, columns), jnp.bfloat16),
        compiler_params=pltpu.CompilerParams(vmem_limit_bytes=40 << 20),
        cost_estimate=pl.CostEstimate(flops=words * words * columns, bytes_accessed=words * columns, transcendentals=0),
        name="attend_back",
    )(length, q, k, v, pull, totals)


def lane_moves(sizes, wide):
    moves, start, channel = [], 0, 0
    for size in sizes:
        for device in range(wide):
            moves.append((device, start, channel + device * size, size))
        start += size
        channel += size * wide
    return moves


def shifted(value, lane_from, lane_to):
    shift = (lane_to - lane_from) % value.shape[1]
    return pltpu.roll(value, shift, 1) if shift else value


def row_places(row, shape, lanes):
    count, size = shape
    places = []
    for i in range(count):
        for low in range(0, size, lanes):
            places.append((row, i, low, min(low + lanes, size)))
            row += 1
    return places


def share_body(sizes, starts, *refs):
    others, out_ref, rest = refs[len(sizes) : -2], refs[-2], refs[-1]
    lanes = out_ref.shape[1]
    start = 0
    for ref, size in zip(refs, sizes):
        rows = ref.shape[1]
        value = ref[...].astype(jnp.float32).T.astype(out_ref.dtype)
        out_ref[:rows, start : start + size] = value
        if rows < TAP:
            out_ref[rows:TAP, start : start + size] = jnp.zeros((TAP - rows, size), out_ref.dtype)
        start += size
    rest[...] = jnp.zeros_like(rest)
    for ref, row in zip(others, starts):
        value = ref[...].astype(jnp.float32)
        for target, i, low, high in row_places(row - TAP, ref.shape, lanes):
            rest[target : target + 1, : high - low] = value[i : i + 1, low:high]
    out_ref[TAP:, :] = rest[...].astype(out_ref.dtype)


def make_share(kernels, others, starts, rows, lanes):
    sizes = [kernel.shape[1] for kernel in kernels]
    return pl.pallas_call(
        functools.partial(share_body, sizes, starts),
        out_shape=jax.ShapeDtypeStruct((rows, lanes), jnp.bfloat16),
        scratch_shapes=[pltpu.VMEM((rows - TAP, lanes), jnp.float32)],
        name="make_share",
    )(*[kernel.T for kernel in kernels], *others)


def kernel_body(sizes, wide, all_ref, out_ref):
    filters = out_ref.shape[1]
    lanes = all_ref.shape[2]
    width = min(lanes, 128)
    lane = lax.broadcasted_iota(jnp.int32, (TAP, 128), 1)
    tiles = [None] * (filters // 128)
    for device, start, channel, size in lane_moves(sizes, wide):
        low = start // width * width
        value = all_ref[device, :TAP, low : low + width].astype(jnp.float32)
        if width < 128:
            value = jnp.concatenate([value, jnp.zeros((TAP, 128 - width), jnp.float32)], axis=1)
        value = shifted(value, start - low, channel % 128)
        tile = channel // 128
        inside = (lane >= channel % 128) & (lane < channel % 128 + size)
        tiles[tile] = jnp.where(inside, value, 0.0 if tiles[tile] is None else tiles[tile])
    for i, tile in enumerate(tiles):
        out_ref[:TAP, i * 128 : (i + 1) * 128] = tile.astype(jnp.bfloat16)
    row = lax.broadcasted_iota(jnp.int32, (KROWS - TAP, filters), 0)
    channel = lax.broadcasted_iota(jnp.int32, (KROWS - TAP, filters), 1)
    below = jnp.zeros((KROWS - TAP, filters), jnp.float32)
    start = 0
    for i, size in enumerate(sizes):
        inside = (row == i + 1) & (channel >= start) & (channel < start + size * wide)
        below = jnp.where(inside, 1.0, below)
        start += size * wide
    biases = jnp.concatenate([all_ref[d, TAP : TAP + 16, :].astype(jnp.float32)[:1] for d in range(wide)], axis=1)
    out_ref[TAP:, :] = jnp.where(row == 0, biases, below).astype(jnp.bfloat16)


def make_kernel(everyone, sizes):
    wide, _, lanes = everyone.shape
    return pl.pallas_call(
        functools.partial(kernel_body, sizes, wide),
        out_shape=jax.ShapeDtypeStruct((KROWS, wide * lanes), jnp.bfloat16),
        name="make_kernel",
    )(everyone)


def shares_body(sizes, wide, starts, grad_ref, *refs):
    others, late_ref, out_ref, rest = refs[:-3], refs[-3], refs[-2], refs[-1]
    lanes = out_ref.shape[2]
    width = min(lanes, 128)
    lane = lax.broadcasted_iota(jnp.int32, (TAP, 128), 1)
    tiles = {}
    for device, start, channel, size in lane_moves(sizes, wide):
        source = grad_ref[:TAP, channel // 128 * 128 : channel // 128 * 128 + 128]
        low = start // width * width
        value = shifted(source, channel % 128, start - low)
        inside = (lane >= start - low) & (lane < start - low + size)
        tiles[device, low] = jnp.where(inside, value, tiles.get((device, low), 0.0))
    for (device, low), tile in tiles.items():
        out_ref[device, :TAP, low : low + width] = tile[:, :width].astype(jnp.bfloat16)
    values = [ref[...] for ref in others]
    rest[...] = jnp.zeros_like(rest)
    early = rest.shape[0] - late_ref.shape[1]
    for device in range(wide):
        rest[:1, :] = grad_ref[TAP : TAP + 8, device * lanes : (device + 1) * lanes][:1]
        for value, row in zip(values, starts):
            count, size = value.shape[0], value.shape[1] // wide
            for target, i, low, high in row_places(row - TAP, (count, size), lanes):
                rest[target : target + 1, : high - low] = value[i : i + 1, device * size + low : device * size + high]
        rest[early:, :] = late_ref[device]
        out_ref[device, TAP:, :] = rest[...].astype(jnp.bfloat16)


def make_shares(grad, others, late, sizes, starts, rows):
    wide, _, lanes = late.shape
    return pl.pallas_call(
        functools.partial(shares_body, sizes, wide, starts),
        out_shape=jax.ShapeDtypeStruct((wide, rows, lanes), jnp.bfloat16),
        scratch_shapes=[pltpu.VMEM((rows - TAP, lanes), jnp.float32)],
        name="make_shares",
    )(grad, *others, late)


def apart_body(sizes, kernel_rows, starts, first, second_ref, *outs):
    total = first[...] + second_ref[...].astype(jnp.float32)
    lanes = total.shape[1]
    width = min(lanes, 128)
    start = 0
    for ref, size, rows in zip(outs, sizes, kernel_rows):
        low = start // width * width
        tile = total[:128, low : low + width]
        if width < 128:
            tile = jnp.concatenate([tile, jnp.zeros((128, 128 - width), jnp.float32)], axis=1)
        tile = shifted(tile, start - low, 0)
        ref[...] = tile[:rows, :size] if size == 128 else tile.T[:size, :rows]
        start += size
    for ref, row in zip(outs[len(sizes) :], starts):
        for source, i, low, high in row_places(row, ref.shape, lanes):
            ref[i : i + 1, low:high] = total[source : source + 1, : high - low]


def take_apart(first, second, sizes, kernel_rows, starts, shapes):
    kernels = [(rows, size) if size == 128 else (size, rows) for rows, size in zip(kernel_rows, sizes)]
    outs = pl.pallas_call(
        functools.partial(apart_body, sizes, kernel_rows, starts),
        out_shape=[jax.ShapeDtypeStruct(shape, jnp.float32) for shape in kernels + shapes],
        name="take_apart",
    )(first, second)
    return [out if i >= len(sizes) or sizes[i] == 128 else out.T for i, out in enumerate(outs)]


def core_swap(value, wide):
    return lax.ppermute(value, "wide", [(i, i ^ 1) for i in range(wide)])


def chip_shift(value, wide, step):
    return lax.ppermute(value, "wide", [(i, (i + 2 * step) % wide) for i in range(wide)])


def hop(value, narrow, bit):
    return lax.ppermute(value, "narrow", [(i, i ^ bit) for i in range(narrow)])


def low_bit(mask):
    return mask & -mask


def high_bit(mask):
    return 1 << (mask.bit_length() - 1)


def masks_of(narrow, level):
    return [mask for mask in range(narrow) if bin(mask).count("1") == level]


def levels_of(narrow):
    return range(1, narrow.bit_length())


def spread_level(known, narrow, level):
    for mask in masks_of(narrow, level):
        if level == 1:
            known[mask] = hop(known[0], narrow, mask)
        else:
            high, low = high_bit(mask), low_bit(mask)
            known[mask] = (hop(known[mask ^ high][0], narrow, high), hop(known[mask ^ low][1], narrow, low))


def add_low(left, right):
    return (left.astype(jnp.float32) + right.astype(jnp.float32)).astype(jnp.bfloat16)


def bits_of(narrow, half):
    bits = [1 << i for i in range(narrow.bit_length() - 1)]
    return bits if half else bits[::-1]


def sides(half, count):
    if half:
        return slice(1, count, 2), slice(0, count, 2)
    return slice(count // 2, count), slice(0, count // 2)


def collect_round(terms, narrow, turn):
    following = []
    for half, (parts, arrived) in enumerate(terms):
        leaving, staying = sides(half, parts.shape[0])
        sent = hop(add_low(parts[leaving], arrived[leaving]), narrow, bits_of(narrow, half)[turn])
        following.append((add_low(parts[staying], arrived[staying]), sent))
    return following


def tie(*groups):
    return lax.optimization_barrier(groups)


def own_columns(shards, layer, place, narrow):
    _, rows, columns = shards.shape
    part = columns // 2 // narrow
    return jnp.concatenate(
        [lax.dynamic_slice(shards, (layer, 0, half * (columns // 2) + place * part), (1, rows, part)) for half in range(2)]
    )


def chip_groups(wide):
    return [[2 * chip + core for chip in range(wide // 2)] for core in range(2)]


def gather_chips(own, wide):
    return lax.all_gather(own, "wide", axis=0, tiled=False, axis_index_groups=chip_groups(wide))


def other_chips(value, chip):
    chips = value.shape[0]
    pieces = [
        lax.dynamic_index_in_dim(value, lax.rem(chip + chips - step, chips), 0, keepdims=False) for step in range(1, chips)
    ]
    return jnp.concatenate(pieces, axis=1)


def swap_early(known, narrow, wide):
    return core_swap(jnp.stack([known[mask] for mask in range(narrow) if not mask & (mask - 1)]), wide)


def swap_late(known, narrow, wide):
    far = [jnp.stack(known[mask]) for mask in range(narrow) if mask & (mask - 1)]
    return [core_swap(jnp.stack(far), wide)] if far else []


def own_rows(shard, place, narrow):
    rows, columns = shard.shape
    own = lax.dynamic_slice_in_dim(shard, place * (rows // narrow), rows // narrow, 0)
    return jnp.stack([own[:, : columns // 2], own[:, columns // 2 :]])


def assemble_body(chips, narrow, where_ref, *rest):
    mine, other, (out_ref, sems) = weight_refs(rest, narrow)
    part = out_ref.shape[1] // narrow
    columns = out_ref.shape[2] // 2
    copies = []
    for side, refs in enumerate((mine, other)):
        for mask in range(narrow):
            start = pl.multiple_of((where_ref[0] ^ mask) * part, part)
            for half in range(2):
                for chip in range(chips):
                    source = refs(mask, half).at[chip * part : (chip + 1) * part, :]
                    target = out_ref.at[
                        2 * chip + (where_ref[2] ^ side), pl.ds(start, part), half * columns : (half + 1) * columns
                    ]
                    copies.append(pltpu.make_async_copy(source, target, sems.at[len(copies)]))
    for copy in copies:
        copy.start()
    for copy in copies:
        copy.wait()


def assemble(where, known, other, wide):
    narrow = len(known)
    _, length, columns = known[0].shape
    chips = wide // 2
    flat = jax.tree.leaves(([known[mask] for mask in range(narrow)], other))
    shape = (wide, narrow * length // chips, 2 * columns)
    return pl.pallas_call(
        functools.partial(assemble_body, chips, narrow),
        grid_spec=pltpu.PrefetchScalarGridSpec(
            num_scalar_prefetch=1,
            grid=(1,),
            in_specs=[pl.BlockSpec(memory_space=pl.ANY)] * len(flat),
            out_specs=pl.BlockSpec(shape, lambda i, where: (0, 0, 0)),
            scratch_shapes=[pltpu.SemaphoreType.DMA((4 * narrow * chips,))],
        ),
        out_shape=jax.ShapeDtypeStruct(shape, known[0].dtype),
        compiler_params=pltpu.CompilerParams(vmem_limit_bytes=60 << 20),
        cost_estimate=pl.CostEstimate(flops=0, bytes_accessed=known[0].size, transcendentals=0),
        name="assemble",
    )(where, *flat)


def weight_copies(narrow, layer, where_ref, mask, shard_ref, twin_ref, mine, other, slot_ref, sems):
    rows = shard_ref.shape[1]
    part = slot_ref.shape[2]
    filters = part * narrow
    chips = slot_ref.shape[1] // (2 * rows)
    copies = []
    for half in range(2):
        column = pl.multiple_of(half * filters + (where_ref[0] ^ mask) * part, part)
        for side, (near, far) in enumerate(((shard_ref, mine), (twin_ref, other))):
            for step in range(chips):
                src = near.at[layer, :, pl.ds(column, part)]
                if step:
                    src = far(mask, half).at[(step - 1) * rows : step * rows, :]
                copies.append((src, slot_ref.at[half, pl.ds(block_start(where_ref, side, step, chips, rows), rows), :]))
    return [pltpu.make_async_copy(src, dst, sems.at[i]) for i, (src, dst) in enumerate(copies)]


def block_start(where_ref, side, step, chips, rows):
    block = lax.rem(where_ref[1] + (chips - step), chips) * 2 + (where_ref[2] ^ side)
    return pl.multiple_of(block * rows, rows)


def weights_of_step(narrow, layer, where_ref, shard_ref, twin_ref, mine, other, slots, sems):
    step = pl.program_id(0)

    def copies(mask):
        return weight_copies(
            narrow, layer, where_ref, mask, shard_ref, twin_ref, mine, other, slots.at[mask % 2], sems.at[mask % 2]
        )

    for mask in range(narrow):
        @pl.when(step == mask)
        def _():
            if mask == 0:
                for copy in copies(0):
                    copy.start()
            if mask + 1 < narrow:
                for copy in copies(mask + 1):
                    copy.start()
            for copy in copies(mask):
                copy.wait()
    return slots.at[lax.rem(step, 2)]


def weight_refs(refs, narrow):
    places, twins, count = {}, {}, 0
    near = [mask for mask in range(narrow) if not mask & (mask - 1)]
    far = [mask for mask in range(narrow) if mask & (mask - 1)]
    for mask in range(narrow):
        for half in range(2):
            if mask in far:
                places[mask, half] = refs[count]
                count += 1
            else:
                places[mask, half] = refs[count].at[half]
        if mask in near:
            count += 1
    for group in (near, far):
        for i, mask in enumerate(group):
            for half in range(2):
                twins[mask, half] = refs[count].at[i, half]
        if group:
            count += 1
    return lambda mask, half: places[mask, half], lambda mask, half: twins[mask, half], refs[count:]


def mix_forward_body(narrow, layer, where_ref, low_ref, carry_ref, shift_a_ref, shift_g_ref, shard_ref, twin_ref, *rest):
    mine, other, (next_ref, low_next_ref, a_ref, cdf_ref, gate_ref, slots, sems) = weight_refs(rest, narrow)
    slot = weights_of_step(narrow, layer, where_ref, shard_ref, twin_ref, mine, other, slots, sems)
    low = low_ref[...]
    a = matmul(low, slot[0]) + shift_a_ref[...]
    g = matmul(low, slot[1]) + shift_g_ref[...]
    gate = jax.nn.sigmoid(g)
    cdf = 0.5 * (1.0 + lax.erf(a * ROOT_HALF))
    a_ref[...] = a
    cdf_ref[...] = cdf
    gate_ref[...] = gate
    following = gate * carry_ref[...] + (1.0 - gate) * (a * cdf)
    next_ref[...] = following
    low_next_ref[...] = following.astype(jnp.bfloat16)


def mix_forward(layer, where, low, carry, shift, shard, twin, mine, other):
    narrow = len(mine)
    words, filters = carry.shape
    part = filters // narrow
    flat = jax.tree.leaves((mine, other))
    block = pl.BlockSpec((words, part), lambda i, where: (0, where[0] ^ i))
    return pl.pallas_call(
        functools.partial(mix_forward_body, narrow, layer),
        grid_spec=pltpu.PrefetchScalarGridSpec(
            num_scalar_prefetch=1,
            grid=(narrow,),
            in_specs=[
                pl.BlockSpec((words, filters), lambda i, where: (0, 0)),
                block,
                pl.BlockSpec((1, part), lambda i, where: (0, where[0] ^ i)),
                pl.BlockSpec((1, part), lambda i, where: (0, narrow + (where[0] ^ i))),
            ]
            + [pl.BlockSpec(memory_space=pl.ANY)] * (2 + len(flat)),
            out_specs=[block] * 5,
            scratch_shapes=[
                pltpu.VMEM((2, 2, filters, part), jnp.bfloat16),
                pltpu.SemaphoreType.DMA((2, 4 * (filters // shard.shape[1] // 2))),
            ],
        ),
        out_shape=[
            jax.ShapeDtypeStruct((words, filters), kind) for kind in (jnp.float32, jnp.bfloat16, jnp.float32, jnp.float32, jnp.float32)
        ],
        compiler_params=pltpu.CompilerParams(vmem_limit_bytes=60 << 20),
        cost_estimate=pl.CostEstimate(
            flops=words * filters * filters, bytes_accessed=filters * filters,
            transcendentals=0,
        ),
        name="mix_forward",
    )(where, low, carry, shift, shift, shard, twin, *flat)


def mix_backward_body(narrow, layer, where_ref, low_ref, carry_ref, a_ref, cdf_ref, gate_ref, pull_ref, shard_ref, twin_ref, *rest):
    mine, other, (own_a, own_g, oth_a, oth_g, shift_ref, back_ref, slots, low_t_ref, sems) = weight_refs(rest, narrow)
    slot = weights_of_step(narrow, layer, where_ref, shard_ref, twin_ref, mine, other, slots, sems)

    @pl.when(pl.program_id(0) == 0)
    def _():
        for start in range(0, low_ref.shape[1], 256):
            low_t_ref[start : start + 256, :] = low_ref[:, start : start + 256].T

    a = a_ref[...]
    cdf = cdf_ref[...]
    gate = gate_ref[...]
    pull = pull_ref[...]
    rest_pull = (1.0 - gate) * pull
    pull_a = (rest_pull * (cdf + a * NORMAL_PEAK * jnp.exp(-0.5 * a * a))).astype(jnp.bfloat16)
    pull_g = (rest_pull * gate * (carry_ref[...] - a * cdf)).astype(jnp.bfloat16)
    half_rows = own_a.shape[1]
    rows = shard_ref.shape[1]
    for half, grad in enumerate((pull_a, pull_g)):
        shift_ref[half, :, :] = jnp.sum(grad.astype(jnp.float32), axis=0, keepdims=True)
        for side, out_ref in enumerate(((own_a, own_g)[half], (oth_a, oth_g)[half])):
            for chip in range(half_rows // rows):
                start = pl.multiple_of((2 * chip + (where_ref[2] ^ side)) * rows, rows)
                out_ref[0, chip * rows : (chip + 1) * rows, :] = matmul(
                    low_t_ref[pl.ds(start, rows), :], grad
                ).astype(jnp.bfloat16)
    back = matmul(pull_a, slot[0], CONTRACT_COLS) + matmul(pull_g, slot[1], CONTRACT_COLS)

    @pl.when(pl.program_id(0) == 0)
    def _():
        back_ref[...] = back

    @pl.when(pl.program_id(0) > 0)
    def _():
        back_ref[...] += back

    part = gate.shape[1]
    column = pl.multiple_of((where_ref[0] ^ pl.program_id(0)) * part, part)
    back_ref[:, pl.ds(column, part)] += gate * pull


def mix_backward(layer, where, low, carry, a, cdf, gate, pull, shard, twin, mine, other):
    narrow = len(mine)
    words, filters = carry.shape
    part = filters // narrow
    flat = jax.tree.leaves((mine, other))
    block = pl.BlockSpec((words, part), lambda i, where: (0, where[0] ^ i))
    grad_block = pl.BlockSpec((1, filters // 2, part), lambda i, where: (i, 0, 0))
    grad_shape = jax.ShapeDtypeStruct((narrow, filters // 2, part), jnp.bfloat16)
    return pl.pallas_call(
        functools.partial(mix_backward_body, narrow, layer),
        grid_spec=pltpu.PrefetchScalarGridSpec(
            num_scalar_prefetch=1,
            grid=(narrow,),
            in_specs=[pl.BlockSpec((words, filters), lambda i, where: (0, 0))]
            + [block] * 5
            + [pl.BlockSpec(memory_space=pl.ANY)] * (2 + len(flat)),
            out_specs=[
                *[grad_block] * 4,
                pl.BlockSpec((2, 1, part), lambda i, where: (0, 0, where[0] ^ i)),
                pl.BlockSpec((words, filters), lambda i, where: (0, 0)),
            ],
            scratch_shapes=[
                pltpu.VMEM((2, 2, filters, part), jnp.bfloat16),
                pltpu.VMEM((filters, words), jnp.bfloat16),
                pltpu.SemaphoreType.DMA((2, 4 * (filters // shard.shape[1] // 2))),
            ],
        ),
        out_shape=[
            *[grad_shape] * 4,
            jax.ShapeDtypeStruct((2, 1, filters), jnp.float32),
            jax.ShapeDtypeStruct((words, filters), jnp.float32),
        ],
        compiler_params=pltpu.CompilerParams(vmem_limit_bytes=60 << 20),
        cost_estimate=pl.CostEstimate(
            flops=words * filters * filters, bytes_accessed=filters * filters,
            transcendentals=0,
        ),
        name="mix_backward",
    )(where, low, carry, a, cdf, gate, pull, shard, twin, *flat)


def from_rows(rows, count, size):
    wide, lines, lanes = rows.shape
    value = rows.reshape(wide, count, lines // count * lanes)[:, :, :size]
    return value.transpose(1, 0, 2).reshape(count, wide * size)


def to_rows(value, wide, lanes):
    count, columns = value.shape
    size = columns // wide
    lines = -(-size // lanes)
    value = value.reshape(count, wide, size).transpose(1, 0, 2)
    return jnp.pad(value, ((0, 0), (0, 0), (0, lines * lanes - size))).reshape(wide, count * lines, lanes)


def shards(
    narrow,
    wide,
    lengths,
    char_ids,
    char_counts,
    token_types,
    out_grad,
    char_table,
    conv_1,
    conv_2,
    conv_3,
    conv_4,
    conv_5,
    conv_6,
    conv_7,
    conv_bias,
    highway_weight,
    highway_bias,
    projection,
    position_table,
    type_table,
    embed_gain,
    embed_biases,
    qkv_weight,
    out_weight,
    ff_in,
    ff_in_bias,
    ff_out,
    layer_gains,
    layer_biases,
):
    convs = (conv_1, conv_2, conv_3, conv_4, conv_5, conv_6, conv_7)
    index = lax.axis_index("wide")
    place = lax.axis_index("narrow")
    where = jnp.stack([place, index // 2, index % 2]).astype(jnp.int32)
    lanes = conv_bias.shape[0]
    filters = lanes * wide
    model_width = embed_gain.shape[0] * wide
    vocab = char_table.shape[0] * wide // CDIM

    kernel_sizes = [kernel.shape[1] for kernel in convs]
    kernel_rows = [kernel.shape[0] for kernel in convs]
    early = [conv_bias[None], highway_bias, type_table, embed_gain[None], embed_biases, layer_gains, layer_biases, ff_in_bias[None]]
    late = char_table[None]
    lines = lambda value: value.shape[0] * -(-value.shape[1] // lanes)
    early_count = sum(map(lines, early))
    early_count += -early_count % 8
    late_count = lines(late)
    late_count += -late_count % 8
    late_count += (early_count + late_count) % 16
    small_rows = TAP + early_count + late_count
    starts = [TAP + sum(map(lines, early[:i])) for i in range(len(early))] + [TAP + early_count]
    small_block = make_share(convs, early + [late], starts, small_rows, lanes)
    columns = [own_columns(highway_weight, number, place, narrow) for number in range(2)]
    small_block, columns = tie(small_block, columns)
    everyone = lax.all_gather(small_block, "wide", axis=0, tiled=False)

    kern = make_kernel(everyone, kernel_sizes)
    channels = [size * wide for size in kernel_sizes]
    width_of = jnp.concatenate([jnp.full((1, count), k + 1, jnp.int32) for k, count in enumerate(channels)], axis=1)
    def whole(number, count, size):
        first = starts[number]
        return from_rows(everyone[:, first : first + count * -(-size // lanes)], count, size)

    model_size = embed_gain.shape[0]
    highway_shift = whole(1, 2, highway_bias.shape[1]).astype(jnp.float32)
    vectors = whole(2, 13, model_size).astype(jnp.float32)
    inner_shift = whole(7, 1, ff_in_bias.shape[0]).astype(jnp.float32)
    table = whole(8, 1, char_table.shape[0]).reshape(vocab, CDIM)
    type_vectors, embed_gain_full, embed_shift = vectors[0:2], vectors[2:3], (vectors[3:4], vectors[4:5])
    gain_rows = (vectors[5:6], vectors[6:7])
    shift_rows = [vectors[7 + i : 8 + i] for i in range(6)]

    seq_count, seq_len, char_slots = char_ids.shape
    word_count = seq_count * seq_len
    counts = char_counts.reshape(word_count, 1)
    slots = lax.broadcasted_iota(jnp.int32, (1, char_slots), 1)
    ids = jnp.where(slots < counts, char_ids.reshape(word_count, char_slots), -1)
    row_keep = (
        (lax.broadcasted_iota(jnp.int32, (seq_count, seq_len), 1) < lengths[:, None])
        .astype(jnp.float32)
        .reshape(word_count, 1)
    )
    type_one = (token_types.reshape(word_count, 1) == 1).astype(jnp.float32)

    levels = levels_of(narrow)
    tables = table_turns(table)
    blocks = word_count // CONV_BLOCK

    def stacked_rows(pieces):
        value = jnp.concatenate(pieces, axis=0)
        return jnp.pad(value, ((0, -value.shape[0] % (16 * narrow)), (0, 0)))

    def side_by_side(value):
        return [value[:, i : i + model_width] for i in range(0, value.shape[1], model_width)]

    deep_one = stacked_rows([projection, position_table] + side_by_side(qkv_weight) + [out_weight])
    deep_two = stacked_rows(side_by_side(ff_in) + [ff_out])
    chips = wide // 2
    stacks = [gather_chips(column, wide) for column in columns]
    state = []
    state = conv_forward(0, blocks // 2, ids, counts, tables, kern, state)
    stacks[0], state, deep_two = tie(stacks[0], state, deep_two)
    stacks.append(gather_chips(own_rows(deep_two, place, narrow), wide))
    known = [{0: other_chips(stacks[0], index // 2)}, None]
    spread_level(known[0], narrow, 1)
    state = conv_forward(blocks // 2, blocks - blocks // 2, ids, counts, tables, kern, state)
    known[0], state, stacks[1], deep_one = tie(known[0], state, stacks[1], deep_one)
    for level in levels[1:]:
        spread_level(known[0], narrow, level)
    twin = core_swap(highway_weight, wide)
    other = [swap_early(known[0], narrow, wide)]
    full_one = lax.all_gather(deep_one, "wide", axis=0, tiled=False)
    windows, totals = state
    places = (jnp.maximum(counts - width_of, 0) + 1).astype(jnp.float32)
    pooled = jnp.log(totals / places)
    carried = gelu_curve(pooled)
    low_state = carried.astype(jnp.bfloat16)
    known[0], twin, other, stacks[1], low_state = tie(known[0], twin, other, stacks[1], low_state)
    other += swap_late(known[0], narrow, wide)
    known[1] = {0: other_chips(stacks[1], index // 2)}
    spread_level(known[1], narrow, 1)
    states, low_states, mixes, mixers = [], [], [], []

    def mix(number, carried, low_state, other):
        mine = [known[number][mask] for mask in range(narrow)]
        mixers.append((mine, other))
        low_states.append(low_state)
        states.append(carried)
        carried, low_state, *kept = mix_forward(
            number, where, low_state, carried, highway_shift[number : number + 1], highway_weight, twin, mine, other
        )
        mixes.append(kept)
        return carried, low_state

    carried, low_state = mix(0, carried, low_state, other)
    known[1], carried, low_state = tie(known[1], carried, low_state)
    for level in levels[1:]:
        spread_level(known[1], narrow, level)
    other = [swap_early(known[1], narrow, wide)]
    known[1], low_state, other, stacks[2] = tie(known[1], low_state, other, stacks[2])
    known.append({0: jnp.concatenate([stacks[2][chip] for chip in range(chips)], axis=1)})
    spread_level(known[2], narrow, 1)
    carried, low_top = mix(1, carried, low_state, other + swap_late(known[1], narrow, wide))
    full_one, known[2], low_top = tie(full_one, known[2], low_top)
    for level in levels[1:]:
        spread_level(known[2], narrow, level)
    other = [swap_early(known[2], narrow, wide)]

    def taken(full, sizes):
        pieces, start = [], 0
        for size in sizes:
            pieces.append(full[:, start : start + size].reshape(wide * size, model_width))
            start += size
        return pieces

    deep_rows = qkv_weight.shape[0]
    projection_full, position_full, *qkv_parts, out_full = taken(
        full_one, [projection.shape[0], position_table.shape[0]] + [deep_rows] * 4
    )
    position_rows = jnp.tile(position_full.astype(jnp.float32), (seq_count, 1))
    embed_sum = (
        matmul(low_top, projection_full)
        + embed_shift[0]
        + position_rows
        + type_vectors[0:1] * (1.0 - type_one)
        + type_vectors[1:2] * type_one
    )
    embedded = normalize(embed_sum, embed_gain_full, embed_shift[1])
    low_in = embedded.astype(jnp.bfloat16)
    queries = (matmul(low_in, qkv_parts[0]) + shift_rows[0]).astype(jnp.bfloat16)
    keys = matmul(low_in, qkv_parts[1]).astype(jnp.bfloat16)
    values = (matmul(low_in, qkv_parts[2]) + shift_rows[1]).astype(jnp.bfloat16)
    sequences = [slice(i * seq_len, (i + 1) * seq_len) for i in range(seq_count)]
    attended = [
        attend(lengths[i : i + 1], queries[rows], keys[rows], values[rows]) for i, rows in enumerate(sequences)
    ]
    context = jnp.concatenate([pair[0] for pair in attended], axis=0)
    known[2], other, context = tie(known[2], other, context)
    full_two = assemble(where, known[2], other + swap_late(known[2], narrow, wide), wide)
    *inner_parts, ff_out_full = taken(full_two, [deep_rows] * (ff_in.shape[1] // model_width) + [ff_out.shape[0]])
    ff_in_full = jnp.concatenate(inner_parts, axis=1)
    first_in = embedded + matmul(context, out_full) + shift_rows[2]
    first_out = normalize(first_in, gain_rows[0], shift_rows[3])
    low_first = first_out.astype(jnp.bfloat16)
    inner_pre = matmul(low_first, ff_in_full) + inner_shift
    activated = gelu_curve(inner_pre).astype(jnp.bfloat16)
    second_in = first_out + matmul(activated, ff_out_full) + shift_rows[4]
    final_out = normalize(second_in, gain_rows[1], shift_rows[5])
    hidden_out = (final_out * row_keep).reshape(seq_count, seq_len, -1)

    grad_top = out_grad.reshape(word_count, -1).astype(jnp.float32) * row_keep
    norm_pull = jax.vjp(normalize, second_in, gain_rows[1], shift_rows[5])[1]
    grad_second, grad_gain_two, grad_shift_five = norm_pull(grad_top)
    grad_ffn = grad_second.astype(jnp.bfloat16)
    grad_shift_four = jnp.sum(grad_ffn, axis=0, keepdims=True, dtype=jnp.float32)
    weight_ff_out = matmul(activated, grad_ffn, CONTRACT_ROWS)
    grad_inner = (matmul(grad_ffn, ff_out_full, CONTRACT_COLS) * gelu_slope(inner_pre)).astype(jnp.bfloat16)
    grad_ff_bias = jnp.sum(grad_inner, axis=0, keepdims=True, dtype=jnp.float32)
    weight_ff_in = matmul(low_first, grad_inner, CONTRACT_ROWS)
    grad_first = grad_second + matmul(grad_inner, ff_in_full, CONTRACT_COLS)
    norm_pull = jax.vjp(normalize, first_in, gain_rows[0], shift_rows[3])[1]
    grad_res, grad_gain_one, grad_shift_three = norm_pull(grad_first)
    grad_attn = grad_res.astype(jnp.bfloat16)
    grad_shift_two = jnp.sum(grad_attn, axis=0, keepdims=True, dtype=jnp.float32)
    weight_out = matmul(context, grad_attn, CONTRACT_ROWS)
    grad_context = matmul(grad_attn, out_full, CONTRACT_COLS).astype(jnp.bfloat16)
    grad_proj = jnp.concatenate(
        [
            attend_back(lengths[i : i + 1], queries[rows], keys[rows], values[rows], grad_context[rows], attended[i][1])
            for i, rows in enumerate(sequences)
        ],
        axis=1,
    )
    grad_shift_zero = jnp.sum(grad_proj[0], axis=0, keepdims=True, dtype=jnp.float32)
    grad_shift_one = jnp.sum(grad_proj[2], axis=0, keepdims=True, dtype=jnp.float32)
    weight_qkv = [matmul(low_in, grad_proj[i], CONTRACT_ROWS) for i in range(3)]
    grad_embedded = grad_res
    for i in range(3):
        grad_embedded = grad_embedded + matmul(grad_proj[i], qkv_parts[i], CONTRACT_COLS)
    norm_pull = jax.vjp(normalize, embed_sum, embed_gain_full, embed_shift[1])[1]
    grad_sum, grad_embed_gain, grad_embed_shift = norm_pull(grad_embedded)
    grad_embed = grad_sum.astype(jnp.bfloat16)
    grad_embed_zero = jnp.sum(grad_embed, axis=0, keepdims=True, dtype=jnp.float32)
    grad_position = jnp.sum(grad_embed.reshape(seq_count, seq_len, -1), axis=0, dtype=jnp.float32)
    type_mask = type_one.astype(jnp.bfloat16)
    grad_type_one = jnp.sum(grad_embed * type_mask, axis=0, keepdims=True, dtype=jnp.float32)
    grad_type_zero = jnp.sum(grad_embed * (1 - type_mask), axis=0, keepdims=True, dtype=jnp.float32)
    weight_proj = matmul(low_top, grad_embed, CONTRACT_ROWS)
    grad_carry = matmul(grad_embed, projection_full, CONTRACT_COLS)

    def deep(value):
        rows = value.shape[0] // wide
        value = value.astype(jnp.bfloat16).reshape(wide, rows, value.shape[1])
        return [value[:, :, i : i + model_width] for i in range(0, value.shape[2], model_width)]

    def reduce_wide(values):
        parts = [deep(value) for value in values]
        total = lax.psum_scatter(jnp.concatenate([p for part in parts for p in part], axis=1), "wide", scatter_dimension=0)
        return total, [[p.shape[1] for p in part] for part in parts]

    def split_deep(total, sizes):
        values, start = [], 0
        for part in sizes:
            pieces = []
            for size in part:
                pieces.append(total[start : start + size])
                start += size
            values.append(jnp.concatenate(pieces, axis=1).astype(jnp.float32))
        return values

    first_sum, first_sizes = reduce_wide([weight_ff_out, weight_ff_in])

    shift_high = [None, None]
    mix_starts = [starts[1], starts[1] + (starts[2] - starts[1]) // 2]

    def unmix(number, pull):
        *parts, shift_grad, back = mix_backward(
            number, where, low_states[number], states[number], *mixes[number], pull, highway_weight, twin, *mixers[number]
        )
        shift_high[number] = shift_grad.reshape(1, 2 * filters)
        return parts[:2], parts[2:], back


    def begun(own_part, got):
        return list(zip(own_part, got))

    def send_home(terms):
        blocks = [add_low(parts[0], arrived[0]).reshape(chips, -1, parts.shape[-1]) for parts, arrived in terms]
        return lax.psum_scatter(
            jnp.stack(blocks, axis=1), "wide", scatter_dimension=0, axis_index_groups=chip_groups(wide)
        )

    def laid_out(totals):
        pieces = []
        for half in range(2):
            table = jnp.stack([totals[mask][half] for mask in range(narrow)])
            for block in range(narrow):
                pieces.append(lax.dynamic_index_in_dim(table, place ^ block, 0, keepdims=False))
        return jnp.concatenate(pieces, axis=1).astype(jnp.float32)

    def convolve_back(first, last, state):
        return conv_backward(first, last - first, ids.T, windows, scaled, kern, state)

    rounds = range(narrow.bit_length() - 1)
    rounds = range(narrow.bit_length() - 1)

    def swap_axis(value, turn):
        split = value.shape[0] // 2
        return [hop(value[half * split : (half + 1) * split], narrow, bits_of(narrow, half)[turn]) for half in range(2)]

    def add_swapped(value, arrived):
        return add_low(value, jnp.concatenate(arrived, axis=0))

    own_one, other_one, pull = unmix(1, grad_carry)
    got_one = [core_swap(value, wide) for value in other_one]
    second_parts = [value.astype(jnp.bfloat16) for value in (weight_out, *weight_qkv, weight_proj)]
    got_one, second_parts, pull = tie(got_one, second_parts, pull)
    second_sum, second_sizes = reduce_wide(second_parts + [grad_position])
    terms_one = collect_round(begun(own_one, got_one), narrow, 0)
    staying = [parts for parts, _ in terms_one]
    staying, pull = tie(staying, pull)
    own_zero, other_zero, pull = unmix(0, pull)
    terms_one, own_zero, other_zero, pull = tie(
        [(parts, sent) for parts, (_, sent) in zip(staying, terms_one)], own_zero, other_zero, pull
    )
    got_zero = [core_swap(value, wide) for value in other_zero]
    for turn in rounds[1:]:
        terms_one = collect_round(terms_one, narrow, turn)
    scaled = pull * gelu_slope(pooled) / totals
    terms_one, got_zero, scaled = tie(terms_one, got_zero, scaled)
    home_one = send_home(terms_one)
    terms_zero = collect_round(begun(own_zero, got_zero), narrow, 0)
    state = [jnp.zeros(kern.shape, jnp.float32), jnp.zeros((VROWS, 128), jnp.float32)]
    state = convolve_back(0, blocks // 2, state)
    state, terms_zero = tie(state, terms_zero)
    for turn in rounds[1:]:
        terms_zero = collect_round(terms_zero, narrow, turn)
    state = convolve_back(blocks // 2, blocks * 3 // 4, state)
    state, terms_zero, first_sum, second_sum = tie(state, terms_zero, first_sum, second_sum)
    home_zero = send_home(terms_zero)
    second_sent = swap_axis(second_sum, 0)
    first_sent = swap_axis(first_sum, 0)
    state = convolve_back(blocks * 3 // 4, blocks, state)
    state, home_one, second_sum, second_sent, first_sum, first_sent = tie(
        state, home_one, second_sum, second_sent, first_sum, first_sent
    )
    total_one = {0: home_one}
    spread_level(total_one, narrow, 1)
    first_sum = add_swapped(first_sum, first_sent)
    second_sum = add_swapped(second_sum, second_sent)
    for turn in rounds[1:]:
        first_sum = add_swapped(first_sum, swap_axis(first_sum, turn))
        second_sum = add_swapped(second_sum, swap_axis(second_sum, turn))
    kern_grad, table_grad = state
    table_grad = table_grad[:vocab].reshape(vocab, 8, CDIM).sum(axis=1)
    model_grads = jnp.concatenate(
        [
            grad_type_zero,
            grad_type_one,
            grad_embed_gain,
            grad_embed_zero,
            grad_embed_shift,
            grad_gain_one,
            grad_gain_two,
            grad_shift_zero,
            grad_shift_one,
            grad_shift_two,
            grad_shift_three,
            grad_shift_four,
            grad_shift_five,
        ]
    )
    late_rows = to_rows(table_grad.reshape(1, -1), wide, lanes)
    late_rows = jnp.pad(late_rows, ((0, 0), (0, late_count - late_rows.shape[1]), (0, 0)))
    small_part = make_shares(
        kern_grad, [*shift_high, model_grads, grad_ff_bias], late_rows, kernel_sizes, [*mix_starts, starts[2], starts[7]], small_rows
    ).reshape(chips, 2, -1, lanes)

    def exchange(value, at, bit):
        side = (index // bit) % 2
        got = lax.ppermute(
            lax.dynamic_index_in_dim(value, 1 - side, at, keepdims=False), "wide", [(i, i ^ bit) for i in range(wide)]
        )
        return lax.dynamic_index_in_dim(value, side, at, keepdims=False), got

    kept, got = exchange(small_part, 1, 1)
    got, total_one, home_zero, first_sum, second_sum = tie(got, total_one, home_zero, first_sum, second_sum)
    total_zero = {0: home_zero}
    spread_level(total_zero, narrow, 1)
    for level in levels[1:]:
        spread_level(total_one, narrow, level)
    small_sum = add_low(kept, got)
    bit = wide // 2
    while bit > 1:
        kept, got = exchange(small_sum.reshape(2, -1, *small_sum.shape[1:]), 0, bit)
        small_sum = add_low(kept, got)
        bit //= 2
    total_zero, small_sum = tie(total_zero, small_sum)
    for level in levels[1:]:
        spread_level(total_zero, narrow, level)
    small_sum = small_sum[0].astype(jnp.float32)
    for bit in bits_of(narrow, 0):
        small_got = hop(small_sum.astype(jnp.bfloat16), narrow, bit)
        if bit > 1:
            small_sum = small_sum + small_got.astype(jnp.float32)
    weight_high = [laid_out(total_zero), laid_out(total_one)]
    grad_ff_out_sum, grad_ff_in_sum = split_deep(first_sum, first_sizes)
    grad_out_sum, *grad_qkv_sums, grad_projection_sum, grad_position_sum = split_deep(second_sum, second_sizes)
    grad_qkv_sum = jnp.concatenate(grad_qkv_sums, axis=1)
    *conv_grads, bias_sum, mix_sum, type_sum, gain_sum, norm_sum, gains_sum, biases_sum, inner_sum, table_sum = take_apart(
        small_sum, small_got, kernel_sizes, kernel_rows, starts, [value.shape for value in early + [late]]
    )
    return (
        hidden_out,
        table_sum[0],
        *conv_grads,
        bias_sum[0],
        jnp.stack(weight_high),
        mix_sum,
        grad_projection_sum,
        grad_position_sum,
        type_sum,
        gain_sum[0],
        norm_sum,
        grad_qkv_sum,
        grad_out_sum,
        grad_ff_in_sum,
        inner_sum[0],
        grad_ff_out_sum,
        gains_sum,
        biases_sum,
    )


def solution(mesh):
    in_specs = (
        P(("narrow", "wide")),
        P(("narrow", "wide"), None, None),
        P(("narrow", "wide"), None),
        P(("narrow", "wide"), None),
        P(("narrow", "wide"), None, None),
        P("wide"),
        P(None, "wide"),
        P(None, "wide"),
        P(None, "wide"),
        P(None, "wide"),
        P(None, "wide"),
        P(None, "wide"),
        P(None, "wide"),
        P("wide"),
        P(None, "wide", None),
        P(None, "wide"),
        P("wide", None),
        P("wide", None),
        P(None, "wide"),
        P("wide"),
        P(None, "wide"),
        P("wide", None),
        P("wide", None),
        P("wide", None),
        P("wide"),
        P("wide", None),
        P(None, "wide"),
        P(None, "wide"),
    )
    out_specs = (
        P(("narrow", "wide"), None, None),
        P("wide"),
        P(None, "wide"),
        P(None, "wide"),
        P(None, "wide"),
        P(None, "wide"),
        P(None, "wide"),
        P(None, "wide"),
        P(None, "wide"),
        P("wide"),
        P(None, "wide", None),
        P(None, "wide"),
        P("wide", None),
        P("wide", None),
        P(None, "wide"),
        P("wide"),
        P(None, "wide"),
        P("wide", None),
        P("wide", None),
        P("wide", None),
        P("wide"),
        P("wide", None),
        P(None, "wide"),
        P(None, "wide"),
    )
    run = functools.partial(shards, mesh.shape["narrow"], mesh.shape["wide"])
    return jax.shard_map(run, mesh=mesh, in_specs=in_specs, out_specs=out_specs, check_vma=False)
```

```python
import functools
import math

import jax
import jax.numpy as jnp
from jax import lax
from jax.experimental import pallas as pl
from jax.experimental.pallas import tpu as pltpu
from jax.sharding import PartitionSpec as P

HDIM = 64
CDIM = 16
WCH = 50
TAP = 112
KROWS = 128
MASK_LOW = -1e30
VPAD = 384
VROWS = 272
FLAT = 896
CONV_BLOCK = 128

EPSILON = 1e-06
MASKED_SCORE = -1e30
ROOT_HALF = 0.7071067811865476
NORMAL_PEAK = 0.3989422804014327
CONTRACT_ROWS = (((0,), (0,)), ((), ()))
CONTRACT_COLS = (((1,), (1,)), ((), ()))
INNER_FIRST = (((1,), (0,)), ((), ()))


def gelu_curve(value):
    return 0.5 * value * (1.0 + lax.erf(value * ROOT_HALF))


def gelu_slope(value):
    return 0.5 * (1.0 + lax.erf(value * ROOT_HALF)) + value * NORMAL_PEAK * jnp.exp(
        -0.5 * value * value
    )


def normalize(value, gain, shift):
    average = jnp.mean(value, axis=-1, keepdims=True)
    centred = value - average
    spread = jnp.mean(centred * centred, axis=-1, keepdims=True)
    return centred * lax.rsqrt(spread + EPSILON) * gain + shift


def normalize_back(value, gain, pull):
    centred = value - jnp.mean(value, axis=-1, keepdims=True)
    scale = lax.rsqrt(jnp.mean(centred * centred, axis=-1, keepdims=True) + EPSILON)
    unit = centred * scale
    inner = pull * gain
    grad = scale * (
        inner - jnp.mean(inner, axis=-1, keepdims=True) - unit * jnp.mean(inner * unit, axis=-1, keepdims=True)
    )
    return grad, jnp.sum(pull * unit, axis=0, keepdims=True), jnp.sum(pull, axis=0, keepdims=True)


def matmul(left, right, dims=INNER_FIRST):
    return lax.dot_general(left, right, dims, preferred_element_type=jnp.float32)


def conv_fwd_body(block, filters, held, ids_ref, cnt_ref, table_ref, kern_ref, *rest):
    x_ref, den_ref, flat, hot = rest[held:]
    lane = lax.broadcasted_iota(jnp.int32, (block, VPAD), 1)
    groups = FLAT // 128
    for turn in range(8):
        for g in range(groups):
            slot = 8 * g + turn
            if slot < WCH:
                col = ids_ref[:, slot:slot + 1]
                hot[g * block:(g + 1) * block, :] = (col == lane).astype(jnp.float32).astype(jnp.bfloat16)
            else:
                hot[g * block:(g + 1) * block, :] = jnp.zeros((block, VPAD), jnp.bfloat16)
        found = matmul(hot[...], table_ref[turn])
        for g in range(groups):
            part = found[g * block:(g + 1) * block, :]
            if turn == 0:
                flat[:, g * 128:(g + 1) * 128] = part
            else:
                flat[:, g * 128:(g + 1) * 128] += part
    flat[:, FLAT:] = jnp.zeros((block, 128), jnp.float32)
    lane_x = lax.broadcasted_iota(jnp.int32, (block, KROWS), 1)
    width = lane_x - TAP
    count = jnp.broadcast_to(cnt_ref[...], (block, KROWS))
    reach = jnp.maximum(count, width)
    for place in range(WCH):
        a, r = divmod(place, 8)
        first = flat[:, a * 128:(a + 1) * 128]
        if r:
            second = flat[:, (a + 1) * 128:(a + 2) * 128]
            first = pltpu.roll(first, 128 - 16 * r, 1)
            second = pltpu.roll(second, 128 - 16 * r, 1)
            first = jnp.where(lane_x < 128 - 16 * r, first, second)
        extra = jnp.where(width == 0, 1.0, jnp.where((width <= 7) & (place + width > reach), MASK_LOW, 0.0))
        x_ref[place * block:(place + 1) * block, :] = jnp.where(width < 0, first, extra).astype(jnp.bfloat16)

    step = 4
    den_ref[...] = jnp.zeros_like(den_ref)
    tile = 512

    def piece(start, count_p, lo, hi):
        rows = x_ref[pl.ds(start, count_p * block), :]
        summed = matmul(rows, kern_ref[:, lo:hi])
        e = jnp.exp(summed)
        total = e[:block]
        for i in range(1, count_p):
            total = total + e[i * block:(i + 1) * block]
        den_ref[:, lo:hi] += total

    def chunk(i, carry):
        start = pl.multiple_of(i * step * block, step * block)
        for lo in range(0, filters, tile):
            piece(start, step, lo, lo + tile)
        return carry

    lax.fori_loop(0, 11, chunk, 0)
    for lo in range(0, 1024, tile):
        piece(44 * block, 4, lo, lo + tile)
    piece(48 * block, 2, 0, 256)


def conv_forward(call, count, ids, counts, tables, kern, state):
    block = CONV_BLOCK
    words, filters = ids.shape[0], kern.shape[1]
    return pl.pallas_call(
        functools.partial(conv_fwd_body, block, filters, len(state)),
        grid=(count,),
        in_specs=[
            pl.BlockSpec((block, ids.shape[1]), lambda i: (call + i, 0)),
            pl.BlockSpec((block, 1), lambda i: (call + i, 0)),
            pl.BlockSpec(tables.shape, lambda i: (0, 0, 0)),
            pl.BlockSpec(kern.shape, lambda i: (0, 0)),
        ]
        + [pl.BlockSpec(memory_space=pl.ANY)] * len(state),
        out_specs=[
            pl.BlockSpec((WCH * block, KROWS), lambda i: (call + i, 0)),
            pl.BlockSpec((block, filters), lambda i: (call + i, 0)),
        ],
        out_shape=[
            jax.ShapeDtypeStruct((words * WCH, KROWS), jnp.bfloat16),
            jax.ShapeDtypeStruct((words, filters), jnp.float32),
        ],
        input_output_aliases={4: 0, 5: 1} if state else {},
        scratch_shapes=[
            pltpu.VMEM((block, FLAT + 128), jnp.float32),
            pltpu.VMEM((FLAT // 128 * block, VPAD), jnp.bfloat16),
        ],
        compiler_params=pltpu.CompilerParams(vmem_limit_bytes=60 << 20),
        cost_estimate=pl.CostEstimate(
            flops=count * block * WCH * 32 * filters,
            bytes_accessed=count * block * filters,
            transcendentals=0,
        ),
        name="conv_forward",
    )(ids, counts, tables, kern, *state)


def conv_bwd_body(block, filters, idst_ref, x_ref, ginv_ref, kern_ref, kern_in_ref, table_in_ref, kern_grad_ref, table_grad_ref, gx, flat, hot, part):
    @pl.when(pl.program_id(0) == 0)
    def _():
        kern_grad_ref[...] = kern_in_ref[...]
        table_grad_ref[...] = table_in_ref[...]


    tile = 512
    step = 4

    def piece(start, count_p, lo, hi):
        rows = x_ref[pl.ds(start, count_p * block), :]
        k = kern_ref[:, lo:hi]
        e = jnp.exp(matmul(rows, k))
        scale = ginv_ref[:, lo:hi]
        g = jnp.concatenate([e[i * block:(i + 1) * block] * scale for i in range(count_p)], axis=0).astype(jnp.bfloat16)
        kern_grad_ref[:, lo:hi] += matmul(rows, g, CONTRACT_ROWS)
        return matmul(g, k, CONTRACT_COLS)

    def chunk(i, carry):
        start = pl.multiple_of(i * step * block, step * block)
        total = piece(start, step, 0, tile)
        for lo in range(tile, filters, tile):
            total = total + piece(start, step, lo, lo + tile)
        gx[pl.ds(start, step * block), :] = total
        return carry

    lax.fori_loop(0, 11, chunk, 0)
    gx[44 * block:48 * block, :] = piece(44 * block, 4, 0, 512) + piece(44 * block, 4, 512, 1024)
    gx[48 * block:50 * block, :] = piece(48 * block, 2, 0, 256)

    flat[...] = jnp.zeros_like(flat)
    lane_x = lax.broadcasted_iota(jnp.int32, (block, 128), 1)
    for place in range(WCH):
        a, r = divmod(place, 8)
        value = jnp.where(lane_x < TAP, gx[place * block:(place + 1) * block, :], 0.0)
        if r:
            value = pltpu.roll(value, 16 * r, 1)
            flat[:, a * 128:(a + 1) * 128] += jnp.where(lane_x >= 16 * r, value, 0.0)
            flat[:, (a + 1) * 128:(a + 2) * 128] += jnp.where(lane_x < 16 * r, value, 0.0)
        else:
            flat[:, a * 128:(a + 1) * 128] += value
    groups = FLAT // 128
    for g in range(groups):
        part[g * block:(g + 1) * block, :] = flat[:, g * 128:(g + 1) * 128].astype(jnp.bfloat16)
    sub = lax.broadcasted_iota(jnp.int32, (VROWS, block), 0)
    lane_t = lax.broadcasted_iota(jnp.int32, (VROWS, 128), 1)
    for turn in range(8):
        for g in range(groups):
            slot = 8 * g + turn
            if slot < WCH:
                row = idst_ref[slot:slot + 1, :]
                hot[:, g * block:(g + 1) * block] = (row == sub).astype(jnp.float32).astype(jnp.bfloat16)
            else:
                hot[:, g * block:(g + 1) * block] = jnp.zeros((VROWS, block), jnp.bfloat16)
        found = matmul(hot[...], part[...])
        table_grad_ref[...] += jnp.where((lane_t >= 16 * turn) & (lane_t < 16 * turn + 16), found, 0.0)


def conv_backward(call, count, ids_t, x, ginv, kern, state):
    block = CONV_BLOCK
    filters = ginv.shape[1]
    whole = [pl.BlockSpec(kern.shape, lambda i: (0, 0)), pl.BlockSpec((VROWS, 128), lambda i: (0, 0))]
    return pl.pallas_call(
        functools.partial(conv_bwd_body, block, filters),
        grid=(count,),
        in_specs=[
            pl.BlockSpec((ids_t.shape[0], block), lambda i: (0, call + i)),
            pl.BlockSpec((WCH * block, KROWS), lambda i: (call + i, 0)),
            pl.BlockSpec((block, filters), lambda i: (call + i, 0)),
            pl.BlockSpec(kern.shape, lambda i: (0, 0)),
        ]
        + whole,
        out_specs=whole,
        out_shape=[
            jax.ShapeDtypeStruct(kern.shape, jnp.float32),
            jax.ShapeDtypeStruct((VROWS, 128), jnp.float32),
        ],
        input_output_aliases={4: 0, 5: 1},
        scratch_shapes=[
            pltpu.VMEM((WCH * block, 128), jnp.float32),
            pltpu.VMEM((block, FLAT + 128), jnp.float32),
            pltpu.VMEM((VROWS, FLAT // 128 * block), jnp.bfloat16),
            pltpu.VMEM((FLAT // 128 * block, 128), jnp.bfloat16),
        ],
        compiler_params=pltpu.CompilerParams(vmem_limit_bytes=60 << 20),
        cost_estimate=pl.CostEstimate(
            flops=count * block * WCH * 64 * filters,
            bytes_accessed=count * block * filters,
            transcendentals=0,
        ),
        name="conv_backward",
    )(ids_t, x, ginv, kern, *state)


def table_turns(table):
    padded = jnp.pad(table, ((0, VPAD - table.shape[0]), (0, 0)))
    return jnp.stack([jnp.pad(padded, ((0, 0), (16 * r, 112 - 16 * r))) for r in range(8)])


def head_scores(length_ref, q, k, head):
    words, width = q.shape
    lane = lax.broadcasted_iota(jnp.int32, (words, width), 1)
    inside = (lane >= head * HDIM) & (lane < (head + 1) * HDIM)
    own = jnp.where(inside, q.astype(jnp.float32), 0.0).astype(jnp.bfloat16)
    key = lax.broadcasted_iota(jnp.int32, (words, words), 0)
    scores = matmul(k, own, CONTRACT_COLS) * (1.0 / math.sqrt(HDIM))
    return own, inside, key < length_ref[0], scores


def attend_body(length_ref, q_ref, k_ref, v_ref, context_ref, total_ref):
    q, k, v = q_ref[...], k_ref[...], v_ref[...]
    words, width = q.shape
    row = lax.broadcasted_iota(jnp.int32, (width, words), 0)
    context = jnp.zeros((width, words), jnp.float32)
    for head in range(2):
        _, _, keep, scores = head_scores(length_ref, q, k, head)
        scores = jnp.where(keep, scores, MASKED_SCORE)
        highest = jnp.max(scores, axis=0, keepdims=True)
        exponent = jnp.exp(scores - highest)
        denominator = jnp.sum(exponent, axis=0, keepdims=True)
        weights = (exponent * (1.0 / denominator)).astype(jnp.bfloat16)
        own = matmul(v, weights, CONTRACT_ROWS)
        context = jnp.where(row >= head * HDIM, own, context)
        total_ref[0, head : head + 1, :] = highest + jnp.log(denominator)
    context_ref[...] = context.T.astype(jnp.bfloat16)


def attend_back_body(length_ref, q_ref, k_ref, v_ref, pull_ref, total_ref, grad_ref):
    q, k, v = q_ref[...], k_ref[...], v_ref[...]
    pull = pull_ref[...].astype(jnp.float32)
    words, width = q.shape
    row = lax.broadcasted_iota(jnp.int32, (width, words), 0)
    scale = 1.0 / math.sqrt(HDIM)
    grad_q = jnp.zeros((width, words), jnp.float32)
    grad_k = jnp.zeros((words, width), jnp.float32)
    grad_v = jnp.zeros((words, width), jnp.float32)
    for head in range(2):
        own, inside, keep, scores = head_scores(length_ref, q, k, head)
        weights = jnp.where(keep, jnp.exp(scores - total_ref[0, head : head + 1, :]), 0.0)
        own_pull = jnp.where(inside, pull, 0.0).astype(jnp.bfloat16)
        grad_weights = matmul(v, own_pull, CONTRACT_COLS)
        dots = jnp.sum(weights * grad_weights, axis=0, keepdims=True)
        grad_scores = (weights * (grad_weights - dots)).astype(jnp.bfloat16)
        grad_v = grad_v + matmul(weights.astype(jnp.bfloat16), own_pull)
        grad_k = grad_k + matmul(grad_scores, own)
        grad_q = jnp.where(row >= head * HDIM, matmul(k, grad_scores, CONTRACT_ROWS), grad_q)
    grad_ref[0] = (grad_q.T * scale).astype(jnp.bfloat16)
    grad_ref[1] = (grad_k * scale).astype(jnp.bfloat16)
    grad_ref[2] = grad_v.astype(jnp.bfloat16)


def attention_specs(words, columns):
    return pl.BlockSpec((words, 2 * HDIM), lambda i, length: (0, i)), columns // (2 * HDIM)


def attend(length, q, k, v):
    words, columns = q.shape
    block, pairs = attention_specs(words, columns)
    return pl.pallas_call(
        attend_body,
        grid_spec=pltpu.PrefetchScalarGridSpec(
            num_scalar_prefetch=1,
            grid=(pairs,),
            in_specs=[block] * 3,
            out_specs=[block, pl.BlockSpec((1, 8, words), lambda i, length: (i, 0, 0))],
        ),
        out_shape=[
            jax.ShapeDtypeStruct((words, columns), jnp.bfloat16),
            jax.ShapeDtypeStruct((pairs, 8, words), jnp.float32),
        ],
        compiler_params=pltpu.CompilerParams(vmem_limit_bytes=40 << 20),
        cost_estimate=pl.CostEstimate(flops=words * words * columns, bytes_accessed=words * columns, transcendentals=0),
        name="attend",
    )(length, q, k, v)


def attend_back(length, q, k, v, pull, totals):
    words, columns = q.shape
    block, pairs = attention_specs(words, columns)
    return pl.pallas_call(
        attend_back_body,
        grid_spec=pltpu.PrefetchScalarGridSpec(
            num_scalar_prefetch=1,
            grid=(pairs,),
            in_specs=[block] * 4 + [pl.BlockSpec((1, 8, words), lambda i, length: (i, 0, 0))],
            out_specs=pl.BlockSpec((3, words, 2 * HDIM), lambda i, length: (0, 0, i)),
        ),
        out_shape=jax.ShapeDtypeStruct((3, words, columns), jnp.bfloat16),
        compiler_params=pltpu.CompilerParams(vmem_limit_bytes=40 << 20),
        cost_estimate=pl.CostEstimate(flops=words * words * columns, bytes_accessed=words * columns, transcendentals=0),
        name="attend_back",
    )(length, q, k, v, pull, totals)


def lane_moves(sizes, wide):
    moves, start, channel = [], 0, 0
    for size in sizes:
        for device in range(wide):
            moves.append((device, start, channel + device * size, size))
        start += size
        channel += size * wide
    return moves


def shifted(value, lane_from, lane_to):
    shift = (lane_to - lane_from) % value.shape[1]
    return pltpu.roll(value, shift, 1) if shift else value


def row_places(row, shape, lanes):
    count, size = shape
    places = []
    for i in range(count):
        for low in range(0, size, lanes):
            places.append((row, i, low, min(low + lanes, size)))
            row += 1
    return places


def share_body(sizes, starts, *refs):
    others, out_ref, rest = refs[len(sizes) : -2], refs[-2], refs[-1]
    lanes = out_ref.shape[1]
    start = 0
    for ref, size in zip(refs, sizes):
        rows = ref.shape[1]
        value = ref[...].astype(jnp.float32).T.astype(out_ref.dtype)
        out_ref[:rows, start : start + size] = value
        if rows < TAP:
            out_ref[rows:TAP, start : start + size] = jnp.zeros((TAP - rows, size), out_ref.dtype)
        start += size
    rest[...] = jnp.zeros_like(rest)
    for ref, row in zip(others, starts):
        value = ref[...].astype(jnp.float32)
        for target, i, low, high in row_places(row - TAP, ref.shape, lanes):
            rest[target : target + 1, : high - low] = value[i : i + 1, low:high]
    out_ref[TAP:, :] = rest[...].astype(out_ref.dtype)


def make_share(kernels, others, starts, rows, lanes):
    sizes = [kernel.shape[1] for kernel in kernels]
    return pl.pallas_call(
        functools.partial(share_body, sizes, starts),
        out_shape=jax.ShapeDtypeStruct((rows, lanes), jnp.bfloat16),
        scratch_shapes=[pltpu.VMEM((rows - TAP, lanes), jnp.float32)],
        name="make_share",
    )(*[kernel.T for kernel in kernels], *others)


def kernel_body(sizes, wide, all_ref, out_ref):
    filters = out_ref.shape[1]
    lanes = all_ref.shape[2]
    width = min(lanes, 128)
    lane = lax.broadcasted_iota(jnp.int32, (TAP, 128), 1)
    tiles = [None] * (filters // 128)
    for device, start, channel, size in lane_moves(sizes, wide):
        low = start // width * width
        value = all_ref[device, :TAP, low : low + width].astype(jnp.float32)
        if width < 128:
            value = jnp.concatenate([value, jnp.zeros((TAP, 128 - width), jnp.float32)], axis=1)
        value = shifted(value, start - low, channel % 128)
        tile = channel // 128
        inside = (lane >= channel % 128) & (lane < channel % 128 + size)
        tiles[tile] = jnp.where(inside, value, 0.0 if tiles[tile] is None else tiles[tile])
    for i, tile in enumerate(tiles):
        out_ref[:TAP, i * 128 : (i + 1) * 128] = tile.astype(jnp.bfloat16)
    row = lax.broadcasted_iota(jnp.int32, (KROWS - TAP, filters), 0)
    channel = lax.broadcasted_iota(jnp.int32, (KROWS - TAP, filters), 1)
    below = jnp.zeros((KROWS - TAP, filters), jnp.float32)
    start = 0
    for i, size in enumerate(sizes):
        inside = (row == i + 1) & (channel >= start) & (channel < start + size * wide)
        below = jnp.where(inside, 1.0, below)
        start += size * wide
    biases = jnp.concatenate([all_ref[d, TAP : TAP + 16, :].astype(jnp.float32)[:1] for d in range(wide)], axis=1)
    out_ref[TAP:, :] = jnp.where(row == 0, biases, below).astype(jnp.bfloat16)


def make_kernel(everyone, sizes):
    wide, _, lanes = everyone.shape
    return pl.pallas_call(
        functools.partial(kernel_body, sizes, wide),
        out_shape=jax.ShapeDtypeStruct((KROWS, wide * lanes), jnp.bfloat16),
        name="make_kernel",
    )(everyone)


def shares_body(sizes, wide, starts, grad_ref, *refs):
    others, late_ref, out_ref, rest = refs[:-3], refs[-3], refs[-2], refs[-1]
    lanes = out_ref.shape[2]
    width = min(lanes, 128)
    lane = lax.broadcasted_iota(jnp.int32, (TAP, 128), 1)
    tiles = {}
    for device, start, channel, size in lane_moves(sizes, wide):
        source = grad_ref[:TAP, channel // 128 * 128 : channel // 128 * 128 + 128]
        low = start // width * width
        value = shifted(source, channel % 128, start - low)
        inside = (lane >= start - low) & (lane < start - low + size)
        tiles[device, low] = jnp.where(inside, value, tiles.get((device, low), 0.0))
    for (device, low), tile in tiles.items():
        out_ref[device, :TAP, low : low + width] = tile[:, :width].astype(jnp.bfloat16)
    values = [ref[...] for ref in others]
    rest[...] = jnp.zeros_like(rest)
    early = rest.shape[0] - late_ref.shape[1]
    for device in range(wide):
        rest[:1, :] = grad_ref[TAP : TAP + 8, device * lanes : (device + 1) * lanes][:1]
        for value, row in zip(values, starts):
            count, size = value.shape[0], value.shape[1] // wide
            for target, i, low, high in row_places(row - TAP, (count, size), lanes):
                rest[target : target + 1, : high - low] = value[i : i + 1, device * size + low : device * size + high]
        rest[early:, :] = late_ref[device]
        out_ref[device, TAP:, :] = rest[...].astype(jnp.bfloat16)


def make_shares(grad, others, late, sizes, starts, rows):
    wide, _, lanes = late.shape
    return pl.pallas_call(
        functools.partial(shares_body, sizes, wide, starts),
        out_shape=jax.ShapeDtypeStruct((wide, rows, lanes), jnp.bfloat16),
        scratch_shapes=[pltpu.VMEM((rows - TAP, lanes), jnp.float32)],
        name="make_shares",
    )(grad, *others, late)


def apart_body(sizes, kernel_rows, starts, first, second_ref, *outs):
    total = first[...] + second_ref[...].astype(jnp.float32)
    lanes = total.shape[1]
    width = min(lanes, 128)
    start = 0
    for ref, size, rows in zip(outs, sizes, kernel_rows):
        low = start // width * width
        tile = total[:128, low : low + width]
        if width < 128:
            tile = jnp.concatenate([tile, jnp.zeros((128, 128 - width), jnp.float32)], axis=1)
        tile = shifted(tile, start - low, 0)
        ref[...] = tile[:rows, :size] if size == 128 else tile.T[:size, :rows]
        start += size
    for ref, row in zip(outs[len(sizes) :], starts):
        for source, i, low, high in row_places(row, ref.shape, lanes):
            ref[i : i + 1, low:high] = total[source : source + 1, : high - low]


def take_apart(first, second, sizes, kernel_rows, starts, shapes):
    kernels = [(rows, size) if size == 128 else (size, rows) for rows, size in zip(kernel_rows, sizes)]
    outs = pl.pallas_call(
        functools.partial(apart_body, sizes, kernel_rows, starts),
        out_shape=[jax.ShapeDtypeStruct(shape, jnp.float32) for shape in kernels + shapes],
        name="take_apart",
    )(first, second)
    return [out if i >= len(sizes) or sizes[i] == 128 else out.T for i, out in enumerate(outs)]


def core_swap(value, wide):
    return lax.ppermute(value, "wide", [(i, i ^ 1) for i in range(wide)])


def chip_shift(value, wide, step):
    return lax.ppermute(value, "wide", [(i, (i + 2 * step) % wide) for i in range(wide)])


def hop(value, narrow, bit):
    return lax.ppermute(value, "narrow", [(i, i ^ bit) for i in range(narrow)])


def low_bit(mask):
    return mask & -mask


def high_bit(mask):
    return 1 << (mask.bit_length() - 1)


def masks_of(narrow, level):
    return [mask for mask in range(narrow) if bin(mask).count("1") == level]


def levels_of(narrow):
    return range(1, narrow.bit_length())


def spread_level(known, narrow, level):
    for mask in masks_of(narrow, level):
        if level == 1:
            known[mask] = hop(known[0], narrow, mask)
        else:
            high, low = high_bit(mask), low_bit(mask)
            known[mask] = (hop(known[mask ^ high][0], narrow, high), hop(known[mask ^ low][1], narrow, low))


def add_low(left, right):
    return (left.astype(jnp.float32) + right.astype(jnp.float32)).astype(jnp.bfloat16)


def bits_of(narrow, half):
    bits = [1 << i for i in range(narrow.bit_length() - 1)]
    return bits if half else bits[::-1]


def sides(half, count):
    if half:
        return slice(1, count, 2), slice(0, count, 2)
    return slice(count // 2, count), slice(0, count // 2)


def round_sums(terms):
    sums = []
    for half, (parts, arrived) in enumerate(terms):
        leaving, staying = sides(half, parts.shape[0])
        sums.append((add_low(parts[leaving], arrived[leaving]), add_low(parts[staying], arrived[staying])))
    return sums


def collect_round(terms, narrow, turn):
    return [
        (staying, hop(leaving, narrow, bits_of(narrow, half)[turn]))
        for half, (leaving, staying) in enumerate(round_sums(terms))
    ]


def tie(*groups):
    return lax.optimization_barrier(groups)


def own_columns(shards, layer, place, narrow):
    _, rows, columns = shards.shape
    part = columns // 2 // narrow
    return jnp.concatenate(
        [lax.dynamic_slice(shards, (layer, 0, half * (columns // 2) + place * part), (1, rows, part)) for half in range(2)]
    )


def chip_groups(wide):
    return [[2 * chip + core for chip in range(wide // 2)] for core in range(2)]


def gather_chips(own, wide):
    return lax.all_gather(own, "wide", axis=0, tiled=False, axis_index_groups=chip_groups(wide))


def other_chips(value, chip):
    chips = value.shape[0]
    pieces = [
        lax.dynamic_index_in_dim(value, lax.rem(chip + chips - step, chips), 0, keepdims=False) for step in range(1, chips)
    ]
    return jnp.concatenate(pieces, axis=1)


def swap_early(known, narrow, wide):
    return core_swap(jnp.stack([known[mask] for mask in range(narrow) if not mask & (mask - 1)]), wide)


def swap_late(known, narrow, wide):
    far = [jnp.stack(known[mask]) for mask in range(narrow) if mask & (mask - 1)]
    return [core_swap(jnp.stack(far), wide)] if far else []


def own_rows(shard, place, narrow):
    rows, columns = shard.shape
    own = lax.dynamic_slice_in_dim(shard, place * (rows // narrow), rows // narrow, 0)
    return jnp.stack([own[:, : columns // 2], own[:, columns // 2 :]])


def assemble_body(chips, narrow, where_ref, *rest):
    mine, other, (out_ref, sems) = weight_refs(rest, narrow)
    part = out_ref.shape[1] // narrow
    columns = out_ref.shape[2] // 2
    copies = []
    for side, refs in enumerate((mine, other)):
        for mask in range(narrow):
            start = pl.multiple_of((where_ref[0] ^ mask) * part, part)
            for half in range(2):
                for chip in range(chips):
                    source = refs(mask, half).at[chip * part : (chip + 1) * part, :]
                    target = out_ref.at[
                        2 * chip + (where_ref[2] ^ side), pl.ds(start, part), half * columns : (half + 1) * columns
                    ]
                    copies.append(pltpu.make_async_copy(source, target, sems.at[len(copies)]))
    for copy in copies:
        copy.start()
    for copy in copies:
        copy.wait()


def assemble(where, known, other, wide):
    narrow = len(known)
    _, length, columns = known[0].shape
    chips = wide // 2
    flat = jax.tree.leaves(([known[mask] for mask in range(narrow)], other))
    shape = (wide, narrow * length // chips, 2 * columns)
    return pl.pallas_call(
        functools.partial(assemble_body, chips, narrow),
        grid_spec=pltpu.PrefetchScalarGridSpec(
            num_scalar_prefetch=1,
            grid=(1,),
            in_specs=[pl.BlockSpec(memory_space=pl.ANY)] * len(flat),
            out_specs=pl.BlockSpec(shape, lambda i, where: (0, 0, 0)),
            scratch_shapes=[pltpu.SemaphoreType.DMA((4 * narrow * chips,))],
        ),
        out_shape=jax.ShapeDtypeStruct(shape, known[0].dtype),
        compiler_params=pltpu.CompilerParams(vmem_limit_bytes=60 << 20),
        cost_estimate=pl.CostEstimate(flops=0, bytes_accessed=known[0].size, transcendentals=0),
        name="assemble",
    )(where, *flat)


def weight_copies(narrow, layer, where_ref, mask, shard_ref, twin_ref, mine, other, slot_ref, sems):
    rows = shard_ref.shape[1]
    part = slot_ref.shape[2]
    filters = part * narrow
    chips = slot_ref.shape[1] // (2 * rows)
    copies = []
    for half in range(2):
        column = pl.multiple_of(half * filters + (where_ref[0] ^ mask) * part, part)
        for side, (near, far) in enumerate(((shard_ref, mine), (twin_ref, other))):
            for step in range(chips):
                src = near.at[layer, :, pl.ds(column, part)]
                if step:
                    src = far(mask, half).at[(step - 1) * rows : step * rows, :]
                copies.append((src, slot_ref.at[half, pl.ds(block_start(where_ref, side, step, chips, rows), rows), :]))
    return [pltpu.make_async_copy(src, dst, sems.at[i]) for i, (src, dst) in enumerate(copies)]


def block_start(where_ref, side, step, chips, rows):
    block = lax.rem(where_ref[1] + (chips - step), chips) * 2 + (where_ref[2] ^ side)
    return pl.multiple_of(block * rows, rows)


def weights_of_step(narrow, layer, where_ref, shard_ref, twin_ref, mine, other, slots, sems):
    step = pl.program_id(0)

    def copies(mask):
        return weight_copies(
            narrow, layer, where_ref, mask, shard_ref, twin_ref, mine, other, slots.at[mask % 2], sems.at[mask % 2]
        )

    for mask in range(narrow):
        @pl.when(step == mask)
        def _():
            if mask == 0:
                for copy in copies(0):
                    copy.start()
            if mask + 1 < narrow:
                for copy in copies(mask + 1):
                    copy.start()
            for copy in copies(mask):
                copy.wait()
    return slots.at[lax.rem(step, 2)]


def weight_refs(refs, narrow):
    places, twins, count = {}, {}, 0
    near = [mask for mask in range(narrow) if not mask & (mask - 1)]
    far = [mask for mask in range(narrow) if mask & (mask - 1)]
    for mask in range(narrow):
        for half in range(2):
            if mask in far:
                places[mask, half] = refs[count]
                count += 1
            else:
                places[mask, half] = refs[count].at[half]
        if mask in near:
            count += 1
    for group in (near, far):
        for i, mask in enumerate(group):
            for half in range(2):
                twins[mask, half] = refs[count].at[i, half]
        if group:
            count += 1
    return lambda mask, half: places[mask, half], lambda mask, half: twins[mask, half], refs[count:]


def mix_forward_body(narrow, layer, where_ref, low_ref, carry_ref, shift_a_ref, shift_g_ref, shard_ref, twin_ref, *rest):
    mine, other, (next_ref, low_next_ref, a_ref, cdf_ref, gate_ref, slots, sems) = weight_refs(rest, narrow)
    slot = weights_of_step(narrow, layer, where_ref, shard_ref, twin_ref, mine, other, slots, sems)
    low = low_ref[...]
    a = matmul(low, slot[0]) + shift_a_ref[...]
    g = matmul(low, slot[1]) + shift_g_ref[...]
    gate = jax.nn.sigmoid(g)
    cdf = 0.5 * (1.0 + lax.erf(a * ROOT_HALF))
    a_ref[...] = a
    cdf_ref[...] = cdf
    gate_ref[...] = gate
    following = gate * carry_ref[...] + (1.0 - gate) * (a * cdf)
    next_ref[...] = following
    low_next_ref[...] = following.astype(jnp.bfloat16)


def mix_forward(layer, where, low, carry, shift, shard, twin, mine, other):
    narrow = len(mine)
    words, filters = carry.shape
    part = filters // narrow
    flat = jax.tree.leaves((mine, other))
    block = pl.BlockSpec((words, part), lambda i, where: (0, where[0] ^ i))
    return pl.pallas_call(
        functools.partial(mix_forward_body, narrow, layer),
        grid_spec=pltpu.PrefetchScalarGridSpec(
            num_scalar_prefetch=1,
            grid=(narrow,),
            in_specs=[
                pl.BlockSpec((words, filters), lambda i, where: (0, 0)),
                block,
                pl.BlockSpec((1, part), lambda i, where: (0, where[0] ^ i)),
                pl.BlockSpec((1, part), lambda i, where: (0, narrow + (where[0] ^ i))),
            ]
            + [pl.BlockSpec(memory_space=pl.ANY)] * (2 + len(flat)),
            out_specs=[block] * 5,
            scratch_shapes=[
                pltpu.VMEM((2, 2, filters, part), jnp.bfloat16),
                pltpu.SemaphoreType.DMA((2, 4 * (filters // shard.shape[1] // 2))),
            ],
        ),
        out_shape=[
            jax.ShapeDtypeStruct((words, filters), kind) for kind in (jnp.float32, jnp.bfloat16, jnp.float32, jnp.float32, jnp.float32)
        ],
        compiler_params=pltpu.CompilerParams(vmem_limit_bytes=60 << 20),
        cost_estimate=pl.CostEstimate(
            flops=words * filters * filters, bytes_accessed=filters * filters,
            transcendentals=0,
        ),
        name="mix_forward",
    )(where, low, carry, shift, shift, shard, twin, *flat)


def mix_grad_body(rows, where_ref, low_ref, carry_ref, a_ref, cdf_ref, gate_ref, pull_ref, *rest):
    own_a, own_g, oth_a, oth_g, shift_ref, grads_ref, low_t_ref = rest

    @pl.when(pl.program_id(0) == 0)
    def _():
        for start in range(0, low_ref.shape[1], 256):
            low_t_ref[start : start + 256, :] = low_ref[:, start : start + 256].T

    a = a_ref[...]
    cdf = cdf_ref[...]
    gate = gate_ref[...]
    rest_pull = (1.0 - gate) * pull_ref[...]
    pull_a = (rest_pull * (cdf + a * NORMAL_PEAK * jnp.exp(-0.5 * a * a))).astype(jnp.bfloat16)
    pull_g = (rest_pull * gate * (carry_ref[...] - a * cdf)).astype(jnp.bfloat16)
    half_rows = own_a.shape[1]
    for half, grad in enumerate((pull_a, pull_g)):
        grads_ref[half] = grad
        shift_ref[half, :, :] = jnp.sum(grad.astype(jnp.float32), axis=0, keepdims=True)
        for side, out_ref in enumerate(((own_a, own_g)[half], (oth_a, oth_g)[half])):
            for chip in range(half_rows // rows):
                start = pl.multiple_of((2 * chip + (where_ref[2] ^ side)) * rows, rows)
                out_ref[0, chip * rows : (chip + 1) * rows, :] = matmul(
                    low_t_ref[pl.ds(start, rows), :], grad
                ).astype(jnp.bfloat16)


def mix_grad(where, narrow, rows, low, carry, a, cdf, gate, pull):
    words, filters = carry.shape
    part = filters // narrow
    block = pl.BlockSpec((words, part), lambda i, where: (0, where[0] ^ i))
    grad_block = pl.BlockSpec((1, filters // 2, part), lambda i, where: (i, 0, 0))
    return pl.pallas_call(
        functools.partial(mix_grad_body, rows),
        grid_spec=pltpu.PrefetchScalarGridSpec(
            num_scalar_prefetch=1,
            grid=(narrow,),
            in_specs=[pl.BlockSpec((words, filters), lambda i, where: (0, 0))] + [block] * 5,
            out_specs=[
                *[grad_block] * 4,
                pl.BlockSpec((2, 1, part), lambda i, where: (0, 0, where[0] ^ i)),
                pl.BlockSpec((2, words, part), lambda i, where: (0, 0, where[0] ^ i)),
            ],
            scratch_shapes=[pltpu.VMEM((filters, words), jnp.bfloat16)],
        ),
        out_shape=[
            *[jax.ShapeDtypeStruct((narrow, filters // 2, part), jnp.bfloat16)] * 4,
            jax.ShapeDtypeStruct((2, 1, filters), jnp.float32),
            jax.ShapeDtypeStruct((2, words, filters), jnp.bfloat16),
        ],
        compiler_params=pltpu.CompilerParams(vmem_limit_bytes=60 << 20),
        cost_estimate=pl.CostEstimate(flops=words * filters * part, bytes_accessed=words * filters, transcendentals=0),
        name="mix_grad",
    )(where, low, carry, a, cdf, gate, pull)


def mix_pull_body(narrow, layer, where_ref, grads_ref, gate_ref, pull_ref, shard_ref, twin_ref, *rest):
    mine, other, (back_ref, slots, sems) = weight_refs(rest, narrow)
    slot = weights_of_step(narrow, layer, where_ref, shard_ref, twin_ref, mine, other, slots, sems)
    back = matmul(grads_ref[0], slot[0], CONTRACT_COLS) + matmul(grads_ref[1], slot[1], CONTRACT_COLS)

    @pl.when(pl.program_id(0) == 0)
    def _():
        back_ref[...] = back

    @pl.when(pl.program_id(0) > 0)
    def _():
        back_ref[...] += back

    part = gate_ref.shape[1]
    column = pl.multiple_of((where_ref[0] ^ pl.program_id(0)) * part, part)
    back_ref[:, pl.ds(column, part)] += gate_ref[...] * pull_ref[...]


def mix_pull(layer, where, grads, gate, pull, shard, twin, mine, other):
    narrow = len(mine)
    words, filters = gate.shape
    part = filters // narrow
    flat = jax.tree.leaves((mine, other))
    block = pl.BlockSpec((words, part), lambda i, where: (0, where[0] ^ i))
    return pl.pallas_call(
        functools.partial(mix_pull_body, narrow, layer),
        grid_spec=pltpu.PrefetchScalarGridSpec(
            num_scalar_prefetch=1,
            grid=(narrow,),
            in_specs=[pl.BlockSpec((2, words, part), lambda i, where: (0, 0, where[0] ^ i))]
            + [block] * 2
            + [pl.BlockSpec(memory_space=pl.ANY)] * (2 + len(flat)),
            out_specs=pl.BlockSpec((words, filters), lambda i, where: (0, 0)),
            scratch_shapes=[
                pltpu.VMEM((2, 2, filters, part), jnp.bfloat16),
                pltpu.SemaphoreType.DMA((2, 4 * (filters // shard.shape[1] // 2))),
            ],
        ),
        out_shape=jax.ShapeDtypeStruct((words, filters), jnp.float32),
        compiler_params=pltpu.CompilerParams(vmem_limit_bytes=60 << 20),
        cost_estimate=pl.CostEstimate(flops=words * filters * part, bytes_accessed=words * filters, transcendentals=0),
        name="mix_pull",
    )(where, grads, gate, pull, shard, twin, *flat)


def spread_rows(out_ref, value, row):
    wide = out_ref.shape[0]
    rows = value.shape[0] // wide
    for device in range(wide):
        out_ref[device, row : row + rows, :] = value[device * rows : (device + 1) * rows].astype(jnp.bfloat16)
    return row + rows


def first_body(inner_ref, ffn_ref, first_ref, grad_ref, out_ref):
    columns = out_ref.shape[2]
    row = spread_rows(out_ref, matmul(inner_ref[...], ffn_ref[...], CONTRACT_ROWS), 0)
    for start in range(0, grad_ref.shape[1], columns):
        row = spread_rows(out_ref, matmul(first_ref[...], grad_ref[:, start : start + columns], CONTRACT_ROWS), row)


def first_parts(wide, activated, grad_ffn, low_first, grad_inner):
    words, columns = grad_ffn.shape
    return pl.pallas_call(
        first_body,
        out_shape=jax.ShapeDtypeStruct((wide, 2 * activated.shape[1] // wide, columns), jnp.bfloat16),
        compiler_params=pltpu.CompilerParams(vmem_limit_bytes=60 << 20),
        cost_estimate=pl.CostEstimate(flops=words * columns * columns, bytes_accessed=words * columns, transcendentals=0),
        name="first_parts",
    )(activated, grad_ffn, low_first, grad_inner)


def second_body(context_ref, attn_ref, in_ref, proj_ref, top_ref, embed_ref, position_ref, out_ref):
    row = spread_rows(out_ref, matmul(context_ref[...], attn_ref[...], CONTRACT_ROWS), 0)
    for part in range(3):
        row = spread_rows(out_ref, matmul(in_ref[...], proj_ref[part], CONTRACT_ROWS), row)
    row = spread_rows(out_ref, matmul(top_ref[...], embed_ref[...], CONTRACT_ROWS), row)
    spread_rows(out_ref, position_ref[...], row)


def second_parts(wide, context, grad_attn, low_in, grad_proj, low_top, grad_embed, grad_position):
    words, columns = context.shape
    rows = (4 * columns + low_top.shape[1] + grad_position.shape[0]) // wide
    return pl.pallas_call(
        second_body,
        out_shape=jax.ShapeDtypeStruct((wide, rows, columns), jnp.bfloat16),
        compiler_params=pltpu.CompilerParams(vmem_limit_bytes=60 << 20),
        cost_estimate=pl.CostEstimate(flops=words * columns * columns, bytes_accessed=words * columns, transcendentals=0),
        name="second_parts",
    )(context, grad_attn, low_in, grad_proj, low_top, grad_embed, grad_position)


def from_rows(rows, count, size):
    wide, lines, lanes = rows.shape
    value = rows.reshape(wide, count, lines // count * lanes)[:, :, :size]
    return value.transpose(1, 0, 2).reshape(count, wide * size)


def to_rows(value, wide, lanes):
    count, columns = value.shape
    size = columns // wide
    lines = -(-size // lanes)
    value = value.reshape(count, wide, size).transpose(1, 0, 2)
    return jnp.pad(value, ((0, 0), (0, 0), (0, lines * lanes - size))).reshape(wide, count * lines, lanes)


def shards(
    narrow,
    wide,
    lengths,
    char_ids,
    char_counts,
    token_types,
    out_grad,
    char_table,
    conv_1,
    conv_2,
    conv_3,
    conv_4,
    conv_5,
    conv_6,
    conv_7,
    conv_bias,
    highway_weight,
    highway_bias,
    projection,
    position_table,
    type_table,
    embed_gain,
    embed_biases,
    qkv_weight,
    out_weight,
    ff_in,
    ff_in_bias,
    ff_out,
    layer_gains,
    layer_biases,
):
    convs = (conv_1, conv_2, conv_3, conv_4, conv_5, conv_6, conv_7)
    index = lax.axis_index("wide")
    place = lax.axis_index("narrow")
    where = jnp.stack([place, index // 2, index % 2]).astype(jnp.int32)
    lanes = conv_bias.shape[0]
    filters = lanes * wide
    model_width = embed_gain.shape[0] * wide
    vocab = char_table.shape[0] * wide // CDIM

    kernel_sizes = [kernel.shape[1] for kernel in convs]
    kernel_rows = [kernel.shape[0] for kernel in convs]
    early = [conv_bias[None], highway_bias, type_table, embed_gain[None], embed_biases, layer_gains, layer_biases, ff_in_bias[None]]
    late = char_table[None]
    lines = lambda value: value.shape[0] * -(-value.shape[1] // lanes)
    early_count = sum(map(lines, early))
    early_count += -early_count % 8
    late_count = lines(late)
    late_count += -late_count % 8
    late_count += (early_count + late_count) % 16
    small_rows = TAP + early_count + late_count
    starts = [TAP + sum(map(lines, early[:i])) for i in range(len(early))] + [TAP + early_count]
    small_block = make_share(convs, early + [late], starts, small_rows, lanes)
    columns = [own_columns(highway_weight, number, place, narrow) for number in range(2)]
    small_block, columns = tie(small_block, columns)
    everyone = lax.all_gather(small_block, "wide", axis=0, tiled=False)

    kern = make_kernel(everyone, kernel_sizes)
    channels = [size * wide for size in kernel_sizes]
    width_of = jnp.concatenate([jnp.full((1, count), k + 1, jnp.int32) for k, count in enumerate(channels)], axis=1)
    def whole(number, count, size):
        first = starts[number]
        return from_rows(everyone[:, first : first + count * -(-size // lanes)], count, size)

    model_size = embed_gain.shape[0]
    highway_shift = whole(1, 2, highway_bias.shape[1]).astype(jnp.float32)
    vectors = whole(2, 13, model_size).astype(jnp.float32)
    vectors = [vectors[i] for i in range(13)]
    inner_shift = whole(7, 1, ff_in_bias.shape[0])[0].astype(jnp.float32)
    table = whole(8, 1, char_table.shape[0]).reshape(vocab, CDIM)

    seq_count, seq_len, char_slots = char_ids.shape
    word_count = seq_count * seq_len
    counts = char_counts.reshape(word_count, 1)
    slots = lax.broadcasted_iota(jnp.int32, (1, char_slots), 1)
    ids = jnp.where(slots < counts, char_ids.reshape(word_count, char_slots), -1)
    row_keep = (
        (lax.broadcasted_iota(jnp.int32, (seq_count, seq_len), 1) < lengths[:, None])
        .astype(jnp.float32)
        .reshape(word_count, 1)
    )
    type_one = (token_types.reshape(word_count, 1) == 1).astype(jnp.float32)

    levels = levels_of(narrow)
    tables = table_turns(table)
    blocks = word_count // CONV_BLOCK

    def stacked_rows(pieces):
        value = jnp.concatenate(pieces, axis=0)
        return jnp.pad(value, ((0, -value.shape[0] % (16 * narrow)), (0, 0)))

    def side_by_side(value):
        return [value[:, i : i + model_width] for i in range(0, value.shape[1], model_width)]

    deep_one = stacked_rows([projection, position_table] + side_by_side(qkv_weight) + [out_weight])
    deep_two = stacked_rows(side_by_side(ff_in) + [ff_out])
    chips = wide // 2
    stacks = [gather_chips(column, wide) for column in columns]
    state = []
    state = conv_forward(0, blocks // 2, ids, counts, tables, kern, state)
    stacks[0], state, deep_two = tie(stacks[0], state, deep_two)
    stacks.append(gather_chips(own_rows(deep_two, place, narrow), wide))
    known = [{0: other_chips(stacks[0], index // 2)}, None]
    spread_level(known[0], narrow, 1)
    state = conv_forward(blocks // 2, blocks - blocks // 2, ids, counts, tables, kern, state)
    known[0], state, stacks[1], deep_one = tie(known[0], state, stacks[1], deep_one)
    for level in levels[1:]:
        spread_level(known[0], narrow, level)
    twin = core_swap(highway_weight, wide)
    other = [swap_early(known[0], narrow, wide)]
    full_one = lax.all_gather(deep_one, "wide", axis=0, tiled=False)
    windows, totals = state
    places = (jnp.maximum(counts - width_of, 0) + 1).astype(jnp.float32)
    pooled = jnp.log(totals / places)
    carried = gelu_curve(pooled)
    low_state = carried.astype(jnp.bfloat16)
    known[0], twin, other, stacks[1], low_state = tie(known[0], twin, other, stacks[1], low_state)
    other += swap_late(known[0], narrow, wide)
    known[1] = {0: other_chips(stacks[1], index // 2)}
    spread_level(known[1], narrow, 1)
    states, low_states, mixes, mixers = [], [], [], []

    def mix(number, carried, low_state, other):
        mine = [known[number][mask] for mask in range(narrow)]
        mixers.append((mine, other))
        low_states.append(low_state)
        states.append(carried)
        carried, low_state, *kept = mix_forward(
            number, where, low_state, carried, highway_shift[number : number + 1], highway_weight, twin, mine, other
        )
        mixes.append(kept)
        return carried, low_state

    carried, low_state = mix(0, carried, low_state, other)
    known[1], carried, low_state, vectors, inner_shift = tie(known[1], carried, low_state, vectors, inner_shift)
    type_zero, type_other, embed_gain_full, *embed_shift = vectors[:5]
    gain_rows, shift_rows = vectors[5:7], vectors[7:13]
    for level in levels[1:]:
        spread_level(known[1], narrow, level)
    other = [swap_early(known[1], narrow, wide)]
    known[1], low_state, other, stacks[2] = tie(known[1], low_state, other, stacks[2])
    known.append({0: jnp.concatenate([stacks[2][chip] for chip in range(chips)], axis=1)})
    spread_level(known[2], narrow, 1)
    carried, low_top = mix(1, carried, low_state, other + swap_late(known[1], narrow, wide))
    full_one, known[2], low_top = tie(full_one, known[2], low_top)
    for level in levels[1:]:
        spread_level(known[2], narrow, level)
    other = [swap_early(known[2], narrow, wide)]

    def taken(full, sizes):
        pieces, start = [], 0
        for size in sizes:
            pieces.append(full[:, start : start + size].reshape(wide * size, model_width))
            start += size
        return pieces

    deep_rows = qkv_weight.shape[0]
    projection_full, position_full, *qkv_parts, out_full = taken(
        full_one, [projection.shape[0], position_table.shape[0]] + [deep_rows] * 4
    )
    position_rows = jnp.tile(position_full.astype(jnp.float32), (seq_count, 1))
    embed_sum = (
        matmul(low_top, projection_full)
        + embed_shift[0]
        + position_rows
        + type_zero * (1.0 - type_one)
        + type_other * type_one
    )
    embedded = normalize(embed_sum, embed_gain_full, embed_shift[1])
    low_in = embedded.astype(jnp.bfloat16)
    queries = (matmul(low_in, qkv_parts[0]) + shift_rows[0]).astype(jnp.bfloat16)
    keys = matmul(low_in, qkv_parts[1]).astype(jnp.bfloat16)
    values = (matmul(low_in, qkv_parts[2]) + shift_rows[1]).astype(jnp.bfloat16)
    sequences = [slice(i * seq_len, (i + 1) * seq_len) for i in range(seq_count)]
    attended = [
        attend(lengths[i : i + 1], queries[rows], keys[rows], values[rows]) for i, rows in enumerate(sequences)
    ]
    context = jnp.concatenate([pair[0] for pair in attended], axis=0)
    known[2], other, context = tie(known[2], other, context)
    full_two = assemble(where, known[2], other + swap_late(known[2], narrow, wide), wide)
    *inner_parts, ff_out_full = taken(full_two, [deep_rows] * (ff_in.shape[1] // model_width) + [ff_out.shape[0]])
    ff_in_full = jnp.concatenate(inner_parts, axis=1)
    first_in = embedded + matmul(context, out_full) + shift_rows[2]
    first_out = normalize(first_in, gain_rows[0], shift_rows[3])
    low_first = first_out.astype(jnp.bfloat16)
    inner_pre = matmul(low_first, ff_in_full) + inner_shift
    activated = gelu_curve(inner_pre).astype(jnp.bfloat16)
    second_in = first_out + matmul(activated, ff_out_full) + shift_rows[4]
    final_out = normalize(second_in, gain_rows[1], shift_rows[5])
    hidden_out = (final_out * row_keep).reshape(seq_count, seq_len, -1)

    def reduce_wide(value):
        return lax.psum_scatter(value, "wide", scatter_dimension=0)

    grad_top = out_grad.reshape(word_count, -1).astype(jnp.float32) * row_keep
    grad_second, grad_gain_two, grad_shift_five = normalize_back(second_in, gain_rows[1], grad_top)
    grad_ffn = grad_second.astype(jnp.bfloat16)
    grad_shift_four = jnp.sum(grad_ffn, axis=0, keepdims=True, dtype=jnp.float32)
    grad_inner = (matmul(grad_ffn, ff_out_full, CONTRACT_COLS) * gelu_slope(inner_pre)).astype(jnp.bfloat16)
    grad_ff_bias = jnp.sum(grad_inner, axis=0, keepdims=True, dtype=jnp.float32)
    grad_first = grad_second + matmul(grad_inner, ff_in_full, CONTRACT_COLS)
    grad_res, grad_gain_one, grad_shift_three = normalize_back(first_in, gain_rows[0], grad_first)
    grad_attn = grad_res.astype(jnp.bfloat16)
    grad_shift_two = jnp.sum(grad_attn, axis=0, keepdims=True, dtype=jnp.float32)
    grad_context = matmul(grad_attn, out_full, CONTRACT_COLS).astype(jnp.bfloat16)
    first_packed = first_parts(wide, activated, grad_ffn, low_first, grad_inner)
    first_sizes = [[ff_out.shape[0]], [ff_in.shape[0]] * (ff_in.shape[1] // model_width)]
    first_packed, grad_context = tie(first_packed, grad_context)
    first_sum = reduce_wide(first_packed)
    grad_proj = jnp.concatenate(
        [
            attend_back(lengths[i : i + 1], queries[rows], keys[rows], values[rows], grad_context[rows], attended[i][1])
            for i, rows in enumerate(sequences)
        ],
        axis=1,
    )
    grad_shift_zero = jnp.sum(grad_proj[0], axis=0, keepdims=True, dtype=jnp.float32)
    grad_shift_one = jnp.sum(grad_proj[2], axis=0, keepdims=True, dtype=jnp.float32)
    grad_embedded = grad_res
    for i in range(3):
        grad_embedded = grad_embedded + matmul(grad_proj[i], qkv_parts[i], CONTRACT_COLS)
    grad_sum, grad_embed_gain, grad_embed_shift = normalize_back(embed_sum, embed_gain_full, grad_embedded)
    grad_embed = grad_sum.astype(jnp.bfloat16)
    grad_embed_zero = jnp.sum(grad_embed, axis=0, keepdims=True, dtype=jnp.float32)
    grad_position = jnp.sum(grad_embed.reshape(seq_count, seq_len, -1), axis=0, dtype=jnp.float32)
    type_mask = type_one.astype(jnp.bfloat16)
    grad_type_one = jnp.sum(grad_embed * type_mask, axis=0, keepdims=True, dtype=jnp.float32)
    grad_type_zero = jnp.sum(grad_embed * (1 - type_mask), axis=0, keepdims=True, dtype=jnp.float32)
    grad_carry = matmul(grad_embed, projection_full, CONTRACT_COLS)

    def split_deep(total, sizes):
        values, start = [], 0
        for part in sizes:
            pieces = []
            for size in part:
                pieces.append(total[start : start + size])
                start += size
            values.append(jnp.concatenate(pieces, axis=1).astype(jnp.float32))
        return values

    shift_high = [None, None]
    mix_starts = [starts[1], starts[1] + (starts[2] - starts[1]) // 2]

    def unmix(number, pull):
        *parts, shift_grad, grads = mix_grad(
            where, narrow, highway_weight.shape[1], low_states[number], states[number], *mixes[number], pull
        )
        shift_high[number] = shift_grad.reshape(1, 2 * filters)
        return parts[:2], parts[2:], grads

    def pull_back(number, grads, pull):
        return mix_pull(number, where, grads, mixes[number][2], pull, highway_weight, twin, *mixers[number])

    def begun(own_part, got):
        return list(zip(own_part, got))

    def home_blocks(terms):
        blocks = [add_low(parts[0], arrived[0]).reshape(chips, -1, parts.shape[-1]) for parts, arrived in terms]
        return jnp.stack(blocks, axis=1)

    def send_home(blocks):
        return lax.psum_scatter(blocks, "wide", scatter_dimension=0, axis_index_groups=chip_groups(wide))

    def laid_out(totals):
        pieces = []
        for half in range(2):
            table = jnp.stack([totals[mask][half] for mask in range(narrow)])
            for block in range(narrow):
                pieces.append(lax.dynamic_index_in_dim(table, place ^ block, 0, keepdims=False))
        return jnp.concatenate(pieces, axis=1).astype(jnp.float32)

    def convolve_back(first, count, state):
        return conv_backward(first, count, ids.T, windows, scaled, kern, state)

    def model_rows():
        return jnp.concatenate(
            [
                grad_type_zero,
                grad_type_one,
                grad_embed_gain,
                grad_embed_zero,
                grad_embed_shift,
                grad_gain_one,
                grad_gain_two,
                grad_shift_zero,
                grad_shift_one,
                grad_shift_two,
                grad_shift_three,
                grad_shift_four,
                grad_shift_five,
            ]
        )

    rounds = range(narrow.bit_length() - 1)

    def swap_axis(value, turn):
        split = value.shape[0] // 2
        return [hop(value[half * split : (half + 1) * split], narrow, bits_of(narrow, half)[turn]) for half in range(2)]

    def add_swapped(value, arrived):
        return add_low(value, jnp.concatenate(arrived, axis=0))

    own_one, other_one, grads = unmix(1, grad_carry)
    got_one = [core_swap(value, wide) for value in other_one]
    pull = pull_back(1, grads, grad_carry)
    got_one, pull = tie(got_one, pull)
    terms_one = collect_round(begun(own_one, got_one), narrow, 0)
    staying = [parts for parts, _ in terms_one]
    staying, pull, context = tie(staying, pull, context)
    second_packed = second_parts(wide, context, grad_attn, low_in, grad_proj, low_top, grad_embed, grad_position)
    second_sizes = [[value.shape[0] // wide] for value in (out_full, *qkv_parts, projection_full, position_full)]
    own_zero, other_zero, grads = unmix(0, pull)
    terms_one, own_zero, other_zero, grads, second_packed = tie(
        [(parts, sent) for parts, (_, sent) in zip(staying, terms_one)], own_zero, other_zero, grads, second_packed
    )
    second_sum = reduce_wide(second_packed)
    got_zero = [core_swap(value, wide) for value in other_zero]
    for turn in rounds[1:-1]:
        terms_one = collect_round(terms_one, narrow, turn)
    sums, grads = tie(round_sums(terms_one), grads)
    sent = [hop(leaving, narrow, bits_of(narrow, half)[rounds[-1]]) for half, (leaving, _) in enumerate(sums)]
    scaled = pull_back(0, grads, pull) * gelu_slope(pooled) / totals
    model_grads = model_rows()
    terms_one = [(staying, arrived) for (_, staying), arrived in zip(sums, sent)]
    terms_one, got_zero, scaled, model_grads = tie(terms_one, got_zero, scaled, model_grads)
    blocks_one = home_blocks(terms_one)
    terms_zero = collect_round(begun(own_zero, got_zero), narrow, 0)
    state = [jnp.zeros(kern.shape, jnp.float32), jnp.zeros((VROWS, 128), jnp.float32)]
    state = convolve_back(0, blocks // 2, state)
    state, terms_zero, blocks_one, first_sum, second_sum = tie(state, terms_zero, blocks_one, first_sum, second_sum)
    home_one = send_home(blocks_one)
    for turn in rounds[1:]:
        terms_zero = collect_round(terms_zero, narrow, turn)
    second_sent = swap_axis(second_sum, 0)
    state = convolve_back(blocks // 2, blocks // 4, state)
    state, terms_zero, second_sum, second_sent = tie(state, terms_zero, second_sum, second_sent)
    second_sum = add_swapped(second_sum, second_sent)
    blocks_zero, state = tie(home_blocks(terms_zero), state)
    home_zero = send_home(blocks_zero)
    total_one = {0: home_one}
    spread_level(total_one, narrow, 1)
    for turn in rounds[1:-1]:
        second_sum = add_swapped(second_sum, swap_axis(second_sum, turn))
    second_sent = swap_axis(second_sum, rounds[-1])
    state = convolve_back(blocks * 3 // 4, blocks // 4, state)
    state, total_one, second_sum, second_sent = tie(state, total_one, second_sum, second_sent)
    second_sum = add_swapped(second_sum, second_sent)
    kern_grad, table_grad = state
    table_grad = table_grad[:vocab].reshape(vocab, 8, CDIM).sum(axis=1)
    late_rows = to_rows(table_grad.reshape(1, -1), wide, lanes)
    late_rows = jnp.pad(late_rows, ((0, 0), (0, late_count - late_rows.shape[1]), (0, 0)))
    small_part = make_shares(
        kern_grad, [*shift_high, model_grads, grad_ff_bias], late_rows, kernel_sizes, [*mix_starts, starts[2], starts[7]], small_rows
    ).reshape(chips, 2, -1, lanes)

    def exchange(value, at, bit):
        side = (index // bit) % 2
        got = lax.ppermute(
            lax.dynamic_index_in_dim(value, 1 - side, at, keepdims=False), "wide", [(i, i ^ bit) for i in range(wide)]
        )
        return lax.dynamic_index_in_dim(value, side, at, keepdims=False), got

    def halves(value):
        return value.reshape(2, -1, *value.shape[1:])

    chip_bits = [wide >> i for i in range(1, wide.bit_length() - 1)]
    place_bits = bits_of(narrow, 1)
    kept, got = exchange(small_part, 1, 1)
    first_sent = swap_axis(first_sum, 0)
    for level in levels[1:]:
        spread_level(total_one, narrow, level)
    kept, got, first_sum, first_sent, total_one = tie(kept, got, first_sum, first_sent, total_one)
    small_sum = add_low(kept, got)
    for bit in chip_bits:
        kept, got = exchange(halves(small_sum), 0, bit)
        small_sum = add_low(kept, got)
    first_sum = add_swapped(first_sum, first_sent)
    for turn in rounds[1:-1]:
        first_sum = add_swapped(first_sum, swap_axis(first_sum, turn))
    first_sent = swap_axis(first_sum, rounds[-1])
    small_sum, first_sum, first_sent, home_zero = tie(small_sum, first_sum, first_sent, home_zero)
    first_sum = add_swapped(first_sum, first_sent)
    total_zero = {0: home_zero}
    spread_level(total_zero, narrow, 1)
    small_sum = small_sum[0].astype(jnp.float32)
    for bit in place_bits[:-1]:
        small_sum = small_sum + hop(small_sum.astype(jnp.bfloat16), narrow, bit).astype(jnp.float32)
    small_sum, total_zero = tie(small_sum, total_zero)
    small_got = hop(small_sum.astype(jnp.bfloat16), narrow, place_bits[-1])
    for level in levels[1:]:
        spread_level(total_zero, narrow, level)
    weight_high = [laid_out(total_zero), laid_out(total_one)]
    grad_ff_out_sum, grad_ff_in_sum = split_deep(first_sum, first_sizes)
    grad_out_sum, *grad_qkv_sums, grad_projection_sum, grad_position_sum = split_deep(second_sum, second_sizes)
    grad_qkv_sum = jnp.concatenate(grad_qkv_sums, axis=1)
    *conv_grads, bias_sum, mix_sum, type_sum, gain_sum, norm_sum, gains_sum, biases_sum, inner_sum, table_sum = take_apart(
        small_sum, small_got, kernel_sizes, kernel_rows, starts, [value.shape for value in early + [late]]
    )
    return (
        hidden_out,
        table_sum[0],
        *conv_grads,
        bias_sum[0],
        jnp.stack(weight_high),
        mix_sum,
        grad_projection_sum,
        grad_position_sum,
        type_sum,
        gain_sum[0],
        norm_sum,
        grad_qkv_sum,
        grad_out_sum,
        grad_ff_in_sum,
        inner_sum[0],
        grad_ff_out_sum,
        gains_sum,
        biases_sum,
    )


def solution(mesh):
    in_specs = (
        P(("narrow", "wide")),
        P(("narrow", "wide"), None, None),
        P(("narrow", "wide"), None),
        P(("narrow", "wide"), None),
        P(("narrow", "wide"), None, None),
        P("wide"),
        P(None, "wide"),
        P(None, "wide"),
        P(None, "wide"),
        P(None, "wide"),
        P(None, "wide"),
        P(None, "wide"),
        P(None, "wide"),
        P("wide"),
        P(None, "wide", None),
        P(None, "wide"),
        P("wide", None),
        P("wide", None),
        P(None, "wide"),
        P("wide"),
        P(None, "wide"),
        P("wide", None),
        P("wide", None),
        P("wide", None),
        P("wide"),
        P("wide", None),
        P(None, "wide"),
        P(None, "wide"),
    )
    out_specs = (
        P(("narrow", "wide"), None, None),
        P("wide"),
        P(None, "wide"),
        P(None, "wide"),
        P(None, "wide"),
        P(None, "wide"),
        P(None, "wide"),
        P(None, "wide"),
        P(None, "wide"),
        P("wide"),
        P(None, "wide", None),
        P(None, "wide"),
        P("wide", None),
        P("wide", None),
        P(None, "wide"),
        P("wide"),
        P(None, "wide"),
        P("wide", None),
        P("wide", None),
        P("wide", None),
        P("wide"),
        P("wide", None),
        P(None, "wide"),
        P(None, "wide"),
    )
    run = functools.partial(shards, mesh.shape["narrow"], mesh.shape["wide"])
    return jax.shard_map(run, mesh=mesh, in_specs=in_specs, out_specs=out_specs, check_vma=False)
```
